128 devices in a mesh: rows: 16 (over z_lo, y, core), layers: 8 (over x, z_hi).
Axes of the slice: x: 4, y: 4, z: 4 (z_hi: 2, z_lo: 2; z = z_hi * 2 + z_lo), core: 2. Of those that a mesh axis runs over, the one named last changes fastest.
Arguments:
- queries: bfloat16 [1024, 16, 4096], P('rows', 'layers'), may hold values from -40 to 40
- stored_rows: bfloat16 [16384, 16, 4096], P('rows', 'layers'), may hold values from -6 to 6
- left_inverse: float32 [16, 64, 64], P('layers'), may hold values from -1 to 24
- right_inverse: float32 [16, 64, 64], P('layers'), may hold values from -1 to 24
Outputs:
- scores: float32 [1024, 16384], P('layers', 'rows')
The draws below stay inside these ranges and needn't reach their ends.
All inputs are finite; a program needn't handle non-finite values.
Results may differ from the reference program's by a relative error of at most 0.0029.
Values may be sent and summed in bfloat16 or wider, within the bound.
No kernel may reach another device: no remote copies, remote signals or barrier semaphores. Data moves between devices by JAX's collectives and lax.ppermute only.
A program may use at most 192 MiB of HBM per device.

```python
import jax
import jax.numpy as jnp
from jax import lax

FACTOR = 64
PROJ = 4096
LAYERS = 16
ROWS = 16384
QUERIES = 1024


def factor_block(key, upper):
    key_diag, key_off = jax.random.split(key)
    diag = jnp.exp(jax.random.uniform(key_diag, (LAYERS, FACTOR), jnp.float32) * jnp.log(upper))
    off = jax.random.uniform(key_off, (LAYERS, FACTOR, FACTOR), jnp.float32, -1.0, 1.0) * (0.9 / FACTOR)
    off = 0.5 * (off + jnp.swapaxes(off, 1, 2))
    eye = jnp.eye(FACTOR, dtype=jnp.float32)
    ramp = 1.0 + 2.0 * jnp.arange(LAYERS, dtype=jnp.float32) / max(LAYERS - 1, 1)
    return ramp[:, None, None] * (off * (1.0 - eye) + eye * diag[:, :, None])


def draw_left_inverse(key, part):
    key = jax.random.fold_in(key, 11)
    return factor_block(key, 3.0)


def draw_right_inverse(key, part):
    key = jax.random.fold_in(key, 23)
    return factor_block(key, 3.0)


def draw_queries(key, part):
    key = jax.random.fold_in(key, 37)
    key_base, key_row, key_col = jax.random.split(key, 3)
    base = jnp.clip(jax.random.normal(key_base, (QUERIES, LAYERS, PROJ), jnp.float32), -4.0, 4.0)
    row_spread = 10.0
    row_scale = jnp.exp(jax.random.uniform(key_row, (QUERIES, 1, 1), jnp.float32) * jnp.log(row_spread))
    col_scale = jnp.exp(jax.random.uniform(key_col, (1, LAYERS, PROJ), jnp.float32) * jnp.log(10.0))
    return (base * row_scale * col_scale * 0.1).astype(jnp.bfloat16)


def levels(key, dims, cuts, smallest, top_value):
    loudness = 1.0
    for position, shards_of in cuts:
        draws = jax.random.uniform(jax.random.fold_in(jax.random.fold_in(key, 6), position), (shards_of,), jnp.float32, smallest / len(cuts), top_value / len(cuts))
        loudness = loudness * jnp.repeat(jnp.exp(draws), dims[position] // shards_of).reshape((-1,) + (1,) * (len(dims) - 1 - position))
    return loudness


def normal_values(own_key, dims, deviation, most, cuts=(), held_as=jnp.bfloat16):
    array = jax.random.normal(own_key, dims, jnp.float32) * deviation
    if len(cuts) > 0:
        array = levels(own_key, dims, cuts, -0.22, 0.18) * array
    return jnp.clip(array, min=-most, max=most).astype(held_as)


def setup_inputs(seed: int = 0) -> dict:
    streams_of = jax.random.split(jax.random.key(seed), 5)
    return {
        "queries": draw_queries(jax.random.fold_in(streams_of[4], 71), 0),
        "stored_rows": normal_values(streams_of[1], (ROWS, LAYERS, PROJ), 1.0, 6.0, ((0, 16), (1, 8))),
        "left_inverse": draw_left_inverse(jax.random.fold_in(streams_of[4], 71), 0),
        "right_inverse": draw_right_inverse(jax.random.fold_in(streams_of[4], 71), 0),
    }


EPS = 1e-06

def precondition(block, left, right):
    count = block.shape[0]
    side = left.shape[-1]
    grid = block.astype(jnp.float32).reshape(count, block.shape[1], side, side)
    first = jnp.einsum('lab,nlbc->nlac', left, grid, precision=lax.Precision.HIGHEST)
    second = jnp.einsum('nlac,lcd->nlad', first, right, precision=lax.Precision.HIGHEST)
    return second.reshape(block.shape)

def reference(queries, stored_rows, left_inverse, right_inverse):
    conditioned = precondition(queries, left_inverse, right_inverse).astype(jnp.bfloat16)
    cond_float = conditioned.astype(jnp.float32)
    norms = lax.optimization_barrier(jnp.sum(cond_float * cond_float, axis=(1, 2)))

    def add_layer(layer, total):
        query_part = lax.dynamic_index_in_dim(cond_float, layer, 1, keepdims=False)
        row_part = lax.dynamic_index_in_dim(stored_rows, layer, 1, keepdims=False).astype(jnp.float32)
        return total + jnp.dot(query_part, row_part.T, precision=lax.Precision.HIGHEST, preferred_element_type=jnp.float32)
    raw = lax.fori_loop(0, LAYERS, add_layer, jnp.zeros((QUERIES, ROWS), jnp.float32))
    return raw * lax.rsqrt(norms + EPS)[:, None]
```

```python
import jax
import jax.numpy as jnp
from jax import lax
from jax.sharding import PartitionSpec as P

EPS = 1e-06
BF = jnp.bfloat16
F32 = jnp.float32
PAD = 128

Z, Y, C, X, ZH = 2, 4, 2, 4, 2
SPLIT = 40


def rows_index(z, y, c):
    return (z * Y + y % Y) * C + c


def rows_perm(move):
    pairs = []
    for z in range(Z):
        for y in range(Y):
            for c in range(C):
                pairs.append((rows_index(z, y, c), rows_index(*move(z, y, c))))
    return pairs


UP = rows_perm(lambda z, y, c: (z, y + 1, c))
DOWN = rows_perm(lambda z, y, c: (z, y - 1, c))
ACROSS = rows_perm(lambda z, y, c: (1 - z, y, c))
SIBLING = rows_perm(lambda z, y, c: (z, y, 1 - c))


def whole_perm(move):
    pairs = []
    for z in range(Z):
        for y in range(Y):
            for c in range(C):
                for x in range(X):
                    for zh in range(ZH):
                        to = move(z, y, x, zh)
                        if to is not None:
                            r = rows_index(z, y, c)
                            source = r * X * ZH + x * ZH + zh
                            target = r * X * ZH + (to[0] % X) * ZH + to[1]
                            pairs.append((source, target))
    return pairs


def precondition(block, left, right):
    count = block.shape[0]
    side = left.shape[-1]
    grid = block.astype(F32).reshape(count, block.shape[1], side, side)
    first = jnp.einsum("lab,nlbc->nlac", left, grid, precision=lax.Precision.HIGHEST)
    second = jnp.einsum("nlac,lcd->nlad", first, right, precision=lax.Precision.HIGHEST)
    return second.reshape(block.shape)


def pack(scores, norms):
    high = lax.reduce_precision(norms, 8, 7)
    low = norms - high
    half = PAD // 2
    count = scores.shape[0]
    return jnp.concatenate(
        [
            scores.astype(BF),
            jnp.broadcast_to(high.astype(BF)[:, None], (count, half)),
            jnp.broadcast_to(low.astype(BF)[:, None], (count, half)),
        ],
        axis=1,
    )


def unpack(block):
    wide = block.astype(F32)
    edge = wide.shape[1] - PAD
    return wide[:, :edge], wide[:, edge] + wide[:, edge + PAD // 2]


def per_device(queries, stored_rows, left_inverse, right_inverse):
    row_count = stored_rows.shape[0]
    width = stored_rows.shape[1] * stored_rows.shape[2]
    stored = stored_rows.reshape(row_count, width)
    rows_at = lax.axis_index("rows")
    layers_at = lax.axis_index("layers")
    z, y, core = rows_at // (Y * C), (rows_at // C) % Y, rows_at % C
    x, zh = layers_at // ZH, layers_at % ZH

    def send(value, pairs):
        return lax.ppermute(value, "rows", pairs)

    ready = precondition(queries, left_inverse, right_inverse).astype(BF)
    own = ready.reshape(ready.shape[0], width)
    count = own.shape[0]
    half = count // 2

    def forward(from_below, from_above):
        n = (from_below.shape[0] // 2 + 7) // 8 * 8
        return jnp.concatenate([send(from_below[:n], UP), send(from_above[n:], DOWN)], axis=0)

    a0o, b0o = own[:SPLIT], own[SPLIT:]
    own_m, own_p = send(own, UP), send(own, DOWN)
    a1o = send(a0o, ACROSS)
    b1o = send(b0o, ACROSS)
    a1m, a1p = send(a1o, UP), send(a1o, DOWN)
    own_t = forward(own_m, own_p)
    a1t = forward(a1m, a1p)
    b1m = send(own_m[SPLIT:], ACROSS)
    b1p = send(own_p[SPLIT:], ACROSS)
    b1t = send(own_t[SPLIT:], ACROSS)
    groups = [
        (0, own, a1o, b1o),
        (-1, own_m, a1m, b1m),
        (1, own_p, a1p, b1p),
        (2, own_t, a1t, b1t),
    ]

    total = jnp.zeros((2 * count, row_count), F32)
    total_norms = jnp.zeros((2 * count,), F32)
    for shift, zero, a1, b1 in groups:
        mine = jnp.concatenate([zero, a1, b1], axis=0)
        other = send(mine, SIBLING)
        flat = jnp.concatenate([mine[:count], other[:count], mine[count:], other[count:]], axis=0)
        part = lax.dot_general(
            flat, stored, (((1,), (1,)), ((), ())), preferred_element_type=F32
        )
        widened = flat.astype(F32)
        packed = pack(part, jnp.sum(widened * widened, axis=1))
        here = (y + shift) % Y // 2
        first = 2 * z + here
        second = 2 * (1 - z) + here
        is_end = (x == first) | (x == second)
        swap = jnp.where(is_end, x == first, (x + 1) % X == second)
        zero_block, one_block = packed[: 2 * count], packed[2 * count :]
        u = jnp.where(swap, one_block, zero_block)
        v = jnp.where(swap, zero_block, one_block)

        def ends(zz, yy, xx):
            return xx % 2 == (yy + shift) % Y // 2

        up = whole_perm(lambda zz, yy, xx, hh: None if ends(zz, yy, xx) else (xx + 1, hh))
        down = whole_perm(lambda zz, yy, xx, hh: None if ends(zz, yy, xx) else (xx - 1, hh))
        over = whole_perm(lambda zz, yy, xx, hh: (xx + 2, hh) if ends(zz, yy, xx) else None)
        both = ("rows", "layers")
        got = [lax.ppermute(u, both, up), lax.ppermute(v, both, down), lax.ppermute(u, both, over)]
        score_sum, norm_sum = unpack(v)
        for block in got:
            s, n = unpack(block)
            score_sum = score_sum + s
            norm_sum = norm_sum + n
        final_zh = (y + shift) % Y % 2
        cross = whole_perm(
            lambda zz, yy, xx, hh: (xx, 1 - hh)
            if ends(zz, yy, xx) and hh != (yy + shift) % Y % 2
            else None
        )
        s, n = unpack(lax.ppermute(pack(score_sum, norm_sum), both, cross))
        is_final = is_end & (zh == final_zh)
        total = jnp.where(is_final, score_sum + s, total)
        total_norms = jnp.where(is_final, norm_sum + n, total_norms)
    scaled = total * lax.rsqrt(total_norms + EPS)[:, None]
    return jnp.where(core == 0, scaled, jnp.roll(scaled, count, axis=0))


def solution(mesh):
    in_specs = (
        P("rows", "layers", None),
        P("rows", "layers", None),
        P("layers", None, None),
        P("layers", None, None),
    )
    out_specs = P("layers", "rows")
    return jax.shard_map(
        per_device, mesh=mesh, in_specs=in_specs, out_specs=out_specs, check_vma=False
    )
```

```python
import jax
import jax.numpy as jnp
from jax import lax
from jax.experimental import pallas as pl
from jax.experimental.pallas import tpu as pltpu
from jax.sharding import PartitionSpec as P

EPS = 1e-06
BF = jnp.bfloat16
F32 = jnp.float32
PAD = 128
MIB = 1 << 20

Z, Y, C, X, ZH = 2, 4, 2, 4, 2
BOTH = ("rows", "layers")


def rows_index(z, y, c):
    return (z * Y + y % Y) * C + c


def rows_perm(move):
    pairs = []
    for z in range(Z):
        for y in range(Y):
            for c in range(C):
                pairs.append((rows_index(z, y, c), rows_index(*move(z, y, c))))
    return pairs


UP = rows_perm(lambda z, y, c: (z, y + 1, c))
DOWN = rows_perm(lambda z, y, c: (z, y - 1, c))
OPPOSITE = rows_perm(lambda z, y, c: (z, y + 2, c))
ACROSS = rows_perm(lambda z, y, c: (1 - z, y, c))
SIBLING = rows_perm(lambda z, y, c: (z, y, 1 - c))


def whole_perm(move):
    pairs = []
    for z in range(Z):
        for y in range(Y):
            for c in range(C):
                for x in range(X):
                    for zh in range(ZH):
                        to = move(z, y, x, zh)
                        if to is not None:
                            r = rows_index(z, y, c)
                            source = r * X * ZH + x * ZH + zh
                            target = r * X * ZH + (to[0] % X) * ZH + to[1]
                            pairs.append((source, target))
    return pairs


def norm_columns(norms):
    count = norms.shape[0]
    high = norms.astype(BF).astype(F32)
    low = norms - high
    lane = lax.broadcasted_iota(jnp.int32, (count, PAD), 1)
    return jnp.where(lane < PAD // 2, high, low).astype(BF)


def thirds(value):
    parts = []
    for _ in range(3):
        parts.append(value.astype(BF))
        value = value - parts[-1].astype(F32)
    return parts

def dot(a, b):
    return lax.dot_general(a, b, (((1,), (0,)), ((), ())), preferred_element_type=F32)

def condition_kernel(q, left, right, out, swapped, back, turned_left):
    count, layers, width = q.shape
    side = right.shape[1]
    four = 4 * side
    tiles = width // 128
    row = lax.broadcasted_iota(jnp.int32, (four, four), 0)
    col = lax.broadcasted_iota(jnp.int32, (four, four), 1)
    right_mask = row // side == col // side
    left_mask = row % 128 // 32 == col % 128 // 32
    total = jnp.zeros((count, 128), F32)
    for l in range(layers):
        lanes = jnp.concatenate([right[l]] * 4, axis=1)
        wide_r = jnp.where(right_mask, jnp.concatenate([lanes] * 4, axis=0), 0.0)
        x = q[:, l, :]
        rows = jnp.concatenate([x[:, four * g : four * (g + 1)] for g in range(width // four)], axis=0)
        first = sum(dot(rows, part) for part in reversed(thirds(wide_r)))
        for g in range(width // four):
            for h in range(four // 128):
                swapped[g * (four // 128) + h] = first[count * g : count * (g + 1), 128 * h : 128 * (h + 1)]
        half = side // 2
        def halves(slot):
            return [turned_left[slot, pl.ds(i, half, stride=2), :] for i in range(2)]

        turned_left[0] = jnp.concatenate([left[l]] * 2, axis=1)
        low, high = halves(0)
        turn = jnp.concatenate([low] * 4 + [high] * 4, axis=0).T[:side]
        turned_left[1] = turn[:, :128]
        turned_left[2] = turn[:, 128:]
        low, high = (jnp.concatenate(pair, axis=1) for pair in zip(halves(1), halves(2)))
        wide_l = jnp.where(left_mask, jnp.concatenate([low] * 4 + [high] * 4, axis=0), 0.0)
        stack = []
        for j in range(count // 4):
            block = jnp.concatenate([swapped[:, 4 * j + i, :] for i in range(4)], axis=0).T
            stack.append(jnp.concatenate([block[:side], block[side:]], axis=1))
        turned = thirds(jnp.concatenate(stack, axis=0))
        factor = thirds(wide_l)
        second = dot(turned[1], factor[1]) + dot(turned[0], factor[2]) + dot(turned[2], factor[0])
        second = second + (dot(turned[0], factor[1]) + dot(turned[1], factor[0]))
        second = second + dot(turned[0], factor[0])
        for j in range(count // 4):
            piece = second[side * j : side * (j + 1)]
            block = jnp.concatenate([piece[:, :128], piece[:, 128:]], axis=0).T
            for i in range(4):
                back[4 * j + i] = block[32 * i : 32 * (i + 1)]
        for t in range(tiles):
            done = back[:, t, :].astype(BF)
            out[:, l * width + 128 * t : l * width + 128 * (t + 1)] = done
            wide = done.astype(F32)
            total = total + wide * wide
    out[:, layers * width :] = norm_columns(jnp.sum(total, axis=1, keepdims=True))

def condition(q, left, right, first, count):
    _, layers, width = q.shape
    return pl.pallas_call(
        condition_kernel,
        out_shape=jax.ShapeDtypeStruct((count, layers * width + PAD), BF),
        grid=(1,),
        in_specs=[pl.BlockSpec((count, layers, width), lambda i: (first, 0, 0)),
            pl.BlockSpec(left.shape, lambda i: (0, 0, 0)), pl.BlockSpec(right.shape, lambda i: (0, 0, 0))],
        out_specs=pl.BlockSpec((count, layers * width + PAD), lambda i: (0, 0)),
        scratch_shapes=[pltpu.VMEM((width // 128, count, 128), F32), pltpu.VMEM((count, width // 128, 128), F32), pltpu.VMEM((3, left.shape[1], 128), F32)],
        compiler_params=pltpu.CompilerParams(vmem_limit_bytes=24 * MIB),
        name="condition",
    )(q, left, right)

def score_kernel(place, *refs):
    *pieces, stored, u, v, group = refs
    half = u.shape[0]
    edge = u.shape[1] - PAD
    width = stored.shape[1]
    for i, piece in enumerate(pieces):
        rows = piece.shape[0]
        group[pl.ds(pl.multiple_of(place[i], rows), rows), :] = piece[...]
    part = lax.dot_general(
        group[:, :width], stored[...], (((1,), (1,)), ((), ())), preferred_element_type=F32
    )
    u[:, :edge] = part[:half].astype(BF)
    v[:, :edge] = part[half:].astype(BF)
    u[:, edge:] = group[:half, width:]
    v[:, edge:] = group[half:, width:]


def score_group(place, pieces, stored):
    count, width = stored.shape
    rows = sum(p.shape[0] for p in pieces)
    shape = jax.ShapeDtypeStruct((rows // 2, count + PAD), BF)
    vmem = pl.BlockSpec(memory_space=pltpu.VMEM)
    return pl.pallas_call(
        score_kernel,
        out_shape=(shape, shape),
        in_specs=[pl.BlockSpec(memory_space=pltpu.SMEM)] + [vmem] * (len(pieces) + 1),
        out_specs=(vmem, vmem),
        scratch_shapes=[pltpu.VMEM((rows, width + PAD), BF)],
        compiler_params=pltpu.CompilerParams(vmem_limit_bytes=20 * MIB),
        cost_estimate=pl.CostEstimate(
            flops=2 * rows * width * count, bytes_accessed=2 * count * width, transcendentals=0
        ),
        name="score_group",
    )(place, *pieces, stored)


def sum_kernel(v, a, b, c, keep, onward):
    edge = v.shape[1] - PAD
    total = v[...].astype(F32) + a[...].astype(F32) + b[...].astype(F32) + c[...].astype(F32)
    norms = total[:, edge : edge + 1] + total[:, edge + PAD // 2 : edge + PAD // 2 + 1]
    keep[:, :edge] = total[:, :edge]
    keep[:, edge:] = jnp.broadcast_to(norms, (v.shape[0], PAD))
    onward[:, :edge] = total[:, :edge].astype(BF)
    onward[:, edge:] = norm_columns(norms)


def sum_blocks(v, a, b, c):
    return pl.pallas_call(
        sum_kernel,
        out_shape=(jax.ShapeDtypeStruct(v.shape, F32), jax.ShapeDtypeStruct(v.shape, BF)),
        compiler_params=pltpu.CompilerParams(vmem_limit_bytes=16 * MIB),
        name="sum_blocks",
    )(v, a, b, c)


def finish_kernel(which, *refs):
    *blocks, out, keep, got, sems = refs
    kinds = len(blocks) // 2
    edge = out.shape[1]
    for i in range(kinds):

        @pl.when(which[0] == i)
        def _(i=i):
            one = pltpu.make_async_copy(blocks[i], keep, sems.at[0])
            two = pltpu.make_async_copy(blocks[kinds + i], got, sems.at[1])
            one.start()
            two.start()
            one.wait()
            two.wait()

    more = got[...].astype(F32)
    norms = keep[:, edge : edge + 1] + (
        more[:, edge : edge + 1] + more[:, edge + PAD // 2 : edge + PAD // 2 + 1]
    )
    out[...] = (keep[:, :edge] + more[:, :edge]) * lax.rsqrt(norms + EPS)


def finish(which, keeps, gots):
    rows, width = keeps[0].shape
    return pl.pallas_call(
        finish_kernel,
        out_shape=jax.ShapeDtypeStruct((rows, width - PAD), F32),
        in_specs=[pl.BlockSpec(memory_space=pltpu.SMEM)]
        + [pl.BlockSpec(memory_space=pl.ANY)] * (2 * len(keeps)),
        scratch_shapes=[
            pltpu.VMEM((rows, width), F32),
            pltpu.VMEM((rows, width), BF),
            pltpu.SemaphoreType.DMA((2,)),
        ],
        compiler_params=pltpu.CompilerParams(vmem_limit_bytes=16 * MIB),
        name="finish",
    )(which, *keeps, *gots)


def after(value, *others):
    return lax.optimization_barrier((value, *others))[0]


def per_device(queries, stored_rows, left_inverse, right_inverse):
    row_count = stored_rows.shape[0]
    width = stored_rows.shape[1] * stored_rows.shape[2]
    rows_at = lax.axis_index("rows")
    layers_at = lax.axis_index("layers")
    z, y, core = rows_at // (Y * C), (rows_at // C) % Y, rows_at % C
    x, zh = layers_at // ZH, layers_at % ZH

    def send(value, pairs):
        return lax.ppermute(value, "rows", pairs)

    n = queries.shape[0] // 2
    b0o = condition(queries, left_inverse, right_inverse, 1, n)

    b0m, b0p = send(b0o, UP), send(b0o, DOWN)
    a0o = condition(after(queries, b0o), left_inverse, right_inverse, 0, n)
    a1o = send(a0o, ACROSS)
    stored = after(stored_rows, a0o).reshape(row_count, width)
    a0o = after(a0o, stored)
    a0m, a0p, b1o = send(after(a0o, b0m), UP), send(after(a0o, b0p), DOWN), send(after(b0o, a1o), ACROSS)
    a1m, a1p = send(after(a1o, a0m), UP), send(after(a1o, a0p), DOWN)
    b1m = send(after(b0m, b1o), ACROSS)
    b0t, a0t = send(after(b0m, a1m), UP), send(after(a0p, a1p), DOWN)
    b1p = send(after(b0p, b1m), ACROSS)
    a1t = send(after(a1o, b0t, a0t), OPPOSITE)
    b1t = send(after(b0t, b1p), ACROSS)
    groups = [
        (0, a0o, b0o, a1o, b1o),
        (-1, a0m, b0m, a1m, b1m),
        (1, a0p, b0p, a1p, b1p),
        (2, a0t, b0t, a1t, b1t),
    ]

    keeps, gots = [], []
    which = 0
    for i, (shift, *mine) in enumerate(groups):
        other = [send(piece, SIBLING) for piece in mine]
        here = (y + shift) % Y // 2
        first = 2 * z + here
        second = 2 * (1 - z) + here
        is_end = (x == first) | (x == second)
        swap = jnp.where(is_end, x == first, (x + 1) % X == second).astype(jnp.int32)
        place = []
        for side in (core, 1 - core):
            for block in (swap, 1 - swap):
                place += [4 * n * block + 2 * n * side, 4 * n * block + 2 * n * side + n]
        place = jnp.stack(place).astype(jnp.int32)
        u, v = score_group(place, mine + other, stored)

        def ends(yy, xx):
            return xx % 2 == (yy + shift) % Y // 2

        up = whole_perm(lambda zz, yy, xx, hh: None if ends(yy, xx) else (xx + 1, hh))
        down = whole_perm(lambda zz, yy, xx, hh: None if ends(yy, xx) else (xx - 1, hh))
        over = whole_perm(lambda zz, yy, xx, hh: (xx + 2, hh) if ends(yy, xx) else None)
        keep, onward = sum_blocks(
            v, lax.ppermute(u, BOTH, up), lax.ppermute(v, BOTH, down), lax.ppermute(u, BOTH, over)
        )
        cross = whole_perm(
            lambda zz, yy, xx, hh: (xx, 1 - hh)
            if ends(yy, xx) and hh != (yy + shift) % Y % 2
            else None
        )
        keeps.append(keep)
        gots.append(lax.ppermute(onward, BOTH, cross))
        which = jnp.where(is_end & (zh == (y + shift) % Y % 2), i, which)
    return finish(jnp.reshape(which, (1,)).astype(jnp.int32), keeps, gots)


def solution(mesh):
    in_specs = (
        P("rows", "layers", None),
        P("rows", "layers", None),
        P("layers", None, None),
        P("layers", None, None),
    )
    out_specs = P("layers", "rows")
    return jax.shard_map(
        per_device, mesh=mesh, in_specs=in_specs, out_specs=out_specs, check_vma=False
    )
```

```python
import functools

import jax
import jax.numpy as jnp
from jax import lax
from jax.experimental import pallas as pl
from jax.experimental.pallas import tpu as pltpu
from jax.sharding import PartitionSpec as P

EPS = 1e-06
BF = jnp.bfloat16
F32 = jnp.float32
PAD = 128
MIB = 1 << 20

Z, Y, C, X, ZH = 2, 4, 2, 4, 2
BOTH = ("rows", "layers")


def rows_index(z, y, c):
    return (z * Y + y % Y) * C + c


def rows_perm(move):
    pairs = []
    for z in range(Z):
        for y in range(Y):
            for c in range(C):
                pairs.append((rows_index(z, y, c), rows_index(*move(z, y, c))))
    return pairs


SAME = rows_perm(lambda z, y, c: (z, y ^ 1, c))
OPPOSITE = rows_perm(lambda z, y, c: (z, y - 1 if y % 2 == 0 else y + 1, c))
ACROSS = rows_perm(lambda z, y, c: (1 - z, y, c))
SIBLING = rows_perm(lambda z, y, c: (z, y, 1 - c))


def whole_perm(move):
    pairs = []
    for z in range(Z):
        for y in range(Y):
            for c in range(C):
                for x in range(X):
                    for zh in range(ZH):
                        to = move(z, y, x, zh)
                        if to is not None:
                            r = rows_index(z, y, c)
                            source = r * X * ZH + x * ZH + zh
                            target = r * X * ZH + (to[0] % X) * ZH + to[1]
                            pairs.append((source, target))
    return pairs


def norm_columns(norms):
    count = norms.shape[0]
    high = norms.astype(BF).astype(F32)
    low = norms - high
    lane = lax.broadcasted_iota(jnp.int32, (count, PAD), 1)
    return jnp.where(lane < PAD // 2, high, low).astype(BF)


def thirds(value):
    parts = []
    for _ in range(3):
        parts.append(value.astype(BF))
        value = value - parts[-1].astype(F32)
    return parts

def dot(a, b):
    return lax.dot_general(a, b, (((1,), (0,)), ((), ())), preferred_element_type=F32)

def condition_kernel(q, left, right, out, swapped, back, turned_left):
    count, layers, width = q.shape
    side = right.shape[1]
    four = 4 * side
    tiles = width // 128
    row = lax.broadcasted_iota(jnp.int32, (four, four), 0)
    col = lax.broadcasted_iota(jnp.int32, (four, four), 1)
    right_mask = row // side == col // side
    left_mask = row % 128 // 32 == col % 128 // 32
    total = jnp.zeros((count, 128), F32)
    for l in range(layers):
        lanes = jnp.concatenate([right[l]] * 4, axis=1)
        wide_r = jnp.where(right_mask, jnp.concatenate([lanes] * 4, axis=0), 0.0)
        x = q[:, l, :]
        rows = jnp.concatenate([x[:, four * g : four * (g + 1)] for g in range(width // four)], axis=0)
        first = sum(dot(rows, part) for part in reversed(thirds(wide_r)))
        for g in range(width // four):
            for h in range(four // 128):
                swapped[g * (four // 128) + h] = first[count * g : count * (g + 1), 128 * h : 128 * (h + 1)]
        half = side // 2
        def halves(slot):
            return [turned_left[slot, pl.ds(i, half, stride=2), :] for i in range(2)]

        turned_left[0] = jnp.concatenate([left[l]] * 2, axis=1)
        low, high = halves(0)
        turn = jnp.concatenate([low] * 4 + [high] * 4, axis=0).T[:side]
        turned_left[1] = turn[:, :128]
        turned_left[2] = turn[:, 128:]
        low, high = (jnp.concatenate(pair, axis=1) for pair in zip(halves(1), halves(2)))
        wide_l = jnp.where(left_mask, jnp.concatenate([low] * 4 + [high] * 4, axis=0), 0.0)
        stack = []
        for j in range(count // 4):
            block = jnp.concatenate([swapped[:, 4 * j + i, :] for i in range(4)], axis=0).T
            stack.append(jnp.concatenate([block[:side], block[side:]], axis=1))
        turned = thirds(jnp.concatenate(stack, axis=0))
        factor = thirds(wide_l)
        second = dot(turned[1], factor[1]) + dot(turned[0], factor[2]) + dot(turned[2], factor[0])
        second = second + (dot(turned[0], factor[1]) + dot(turned[1], factor[0]))
        second = second + dot(turned[0], factor[0])
        for j in range(count // 4):
            piece = second[side * j : side * (j + 1)]
            block = jnp.concatenate([piece[:, :128], piece[:, 128:]], axis=0).T
            for i in range(4):
                back[4 * j + i] = block[32 * i : 32 * (i + 1)]
        for t in range(tiles):
            done = back[:, t, :].astype(BF)
            out[:, l * width + 128 * t : l * width + 128 * (t + 1)] = done
            wide = done.astype(F32)
            total = total + wide * wide
    out[:, layers * width :] = norm_columns(jnp.sum(total, axis=1, keepdims=True))

def condition(q, left, right, first, count):
    _, layers, width = q.shape
    return pl.pallas_call(
        condition_kernel,
        out_shape=jax.ShapeDtypeStruct((count, layers * width + PAD), BF),
        grid=(1,),
        in_specs=[pl.BlockSpec((count, layers, width), lambda i: (first, 0, 0)),
            pl.BlockSpec(left.shape, lambda i: (0, 0, 0)), pl.BlockSpec(right.shape, lambda i: (0, 0, 0))],
        out_specs=pl.BlockSpec((count, layers * width + PAD), lambda i: (0, 0)),
        scratch_shapes=[pltpu.VMEM((width // 128, count, 128), F32), pltpu.VMEM((count, width // 128, 128), F32), pltpu.VMEM((3, left.shape[1], 128), F32)],
        compiler_params=pltpu.CompilerParams(vmem_limit_bytes=24 * MIB),
        name="condition",
    )(q, left, right)

def fill(at, place, pieces, group):
    for i, piece in enumerate(pieces):
        rows = piece.shape[0]
        group[pl.ds(pl.multiple_of(place[at + i], 16), rows), :] = piece[...]


def products(group, stored):
    width = stored.shape[1]
    return lax.dot_general(
        group[:, :width], stored[...], (((1,), (1,)), ((), ())), preferred_element_type=F32
    )


def score_kernel(at, place, *refs):
    *pieces, stored, scores, group = refs
    edge = scores.shape[1] - PAD
    fill(at, place, pieces, group)
    scores[:, :edge] = products(group, stored).astype(BF)
    scores[:, edge:] = group[:, stored.shape[1] :]


def deal_kernel(at, deal, place, *refs):
    *pieces, stored, before, o0, o1, o2, o3, group, blocks = refs
    edge = before.shape[1] - PAD
    rows = before.shape[0]
    fill(at, place, pieces, group)
    blocks[:rows] = before[...]
    blocks[rows:, :edge] = products(group, stored).astype(BF)
    blocks[rows:, edge:] = group[:, stored.shape[1] :]
    for j, out in enumerate((o0, o1, o2, o3)):
        start = pl.multiple_of(place[deal + j] * out.shape[0], 128)
        out[...] = blocks[pl.ds(start, out.shape[0]), :]


def score_group(place, at, pieces, stored, before=None, deal=None):
    count, width = stored.shape
    rows = sum(p.shape[0] for p in pieces)
    vmem = pl.BlockSpec(memory_space=pltpu.VMEM)
    scratch = [pltpu.VMEM((rows, width + PAD), BF)]
    shape = jax.ShapeDtypeStruct((rows, count + PAD), BF)
    more = []
    if before is None:
        kernel, name = functools.partial(score_kernel, at), "score_group"
        out, out_specs = shape, vmem
    else:
        kernel, name = functools.partial(deal_kernel, at, deal), "score_and_deal"
        out = [jax.ShapeDtypeStruct((rows // 2, count + PAD), BF)] * 4
        out_specs = [vmem] * 4
        scratch.append(pltpu.VMEM((2 * rows, count + PAD), BF))
        more = [before]
    return pl.pallas_call(
        kernel,
        out_shape=out,
        in_specs=[pl.BlockSpec(memory_space=pltpu.SMEM)] + [vmem] * (len(pieces) + 1 + len(more)),
        out_specs=out_specs,
        scratch_shapes=scratch,
        compiler_params=pltpu.CompilerParams(vmem_limit_bytes=12 * MIB),
        cost_estimate=pl.CostEstimate(
            flops=2 * rows * width * count, bytes_accessed=2 * count * width, transcendentals=0
        ),
        name=name,
    )(place, *pieces, stored, *more)


def sum_kernel(v, a, b, c, keep, onward):
    edge = v.shape[1] - PAD
    total = v[...].astype(F32) + a[...].astype(F32) + b[...].astype(F32) + c[...].astype(F32)
    norms = total[:, edge : edge + 1] + total[:, edge + PAD // 2 : edge + PAD // 2 + 1]
    keep[:, :edge] = total[:, :edge]
    keep[:, edge:] = jnp.broadcast_to(norms, (v.shape[0], PAD))
    onward[:, :edge] = total[:, :edge].astype(BF)
    onward[:, edge:] = norm_columns(norms)


def sum_blocks(blocks):
    shape = blocks[0].shape
    vmem = pl.BlockSpec(memory_space=pltpu.VMEM)
    return pl.pallas_call(
        sum_kernel,
        out_shape=(jax.ShapeDtypeStruct(shape, F32), jax.ShapeDtypeStruct(shape, BF)),
        in_specs=[vmem] * 4,
        out_specs=(vmem, vmem),
        compiler_params=pltpu.CompilerParams(vmem_limit_bytes=6 * MIB),
        name="sum_blocks",
    )(*blocks)


def finish_kernel(at, which, *refs):
    *blocks, out, keep, got, sems = refs
    kinds = len(blocks) // 2
    edge = out.shape[1]
    for i in range(kinds):

        @pl.when(which[at] == i)
        def _(i=i):
            one = pltpu.make_async_copy(blocks[i], keep, sems.at[0])
            two = pltpu.make_async_copy(blocks[kinds + i], got, sems.at[1])
            one.start()
            two.start()
            one.wait()
            two.wait()

    more = got[...].astype(F32)
    norms = keep[:, edge : edge + 1] + (
        more[:, edge : edge + 1] + more[:, edge + PAD // 2 : edge + PAD // 2 + 1]
    )
    out[...] = (keep[:, :edge] + more[:, :edge]) * lax.rsqrt(norms + EPS)


def finish(which, at, keeps, gots):
    rows, width = keeps[0].shape
    return pl.pallas_call(
        functools.partial(finish_kernel, at),
        out_shape=jax.ShapeDtypeStruct((rows, width - PAD), F32),
        in_specs=[pl.BlockSpec(memory_space=pltpu.SMEM)]
        + [pl.BlockSpec(memory_space=pl.ANY)] * (2 * len(keeps)),
        scratch_shapes=[
            pltpu.VMEM((rows, width), F32),
            pltpu.VMEM((rows, width), BF),
            pltpu.SemaphoreType.DMA((2,)),
        ],
        compiler_params=pltpu.CompilerParams(vmem_limit_bytes=4 * MIB),
        name="finish",
    )(which, *keeps, *gots)


def split_kernel(a, b, first, second):
    count = first.shape[0]
    first[...] = a[:count]
    second[...] = b[count:]


def split(a, b, count):
    vmem = pl.BlockSpec(memory_space=pltpu.VMEM)
    return pl.pallas_call(
        split_kernel,
        out_shape=[jax.ShapeDtypeStruct((size, a.shape[1]), a.dtype) for size in (count, b.shape[0] - count)],
        in_specs=[vmem] * 2,
        out_specs=[vmem] * 2,
        compiler_params=pltpu.CompilerParams(vmem_limit_bytes=4 * MIB),
        name="split",
    )(a, b)


def after(value, *others):
    return lax.optimization_barrier((value, *others))[0]


def per_device(queries, stored_rows, left_inverse, right_inverse):
    row_count = stored_rows.shape[0]
    width = stored_rows.shape[1] * stored_rows.shape[2]
    n = queries.shape[0]
    rows_at = lax.axis_index("rows")
    layers_at = lax.axis_index("layers")
    z, y, core = rows_at // (Y * C), (rows_at // C) % Y, rows_at % C
    x, zh = layers_at // ZH, layers_at % ZH
    side = y // 2

    def send(value, pairs, name):
        with jax.named_scope(name):
            return lax.ppermute(value, "rows", pairs)

    def whole(value, move, name):
        with jax.named_scope(name):
            return lax.ppermute(value, BOTH, whole_perm(move))

    def place(rows_of):
        offsets = []
        for at in (core, 1 - core):
            for block, rows in enumerate(rows_of):
                start = 2 * n * block + n * at
                for count in rows:
                    offsets.append(start)
                    start = start + count
        return offsets

    def dealt():
        to = [(x + step) % X for step in (0, 1, 2, 3)]
        return [2 * (t % 2 != side) + (t // 2 != z) for t in to]

    def reduce_batch(blocks, name):
        mine, up, over, down = blocks
        got = [
            whole(up, lambda zz, yy, xx, hh: (xx + 1, hh), "up" + name),
            whole(down, lambda zz, yy, xx, hh: (xx - 1, hh), "down" + name),
            whole(over, lambda zz, yy, xx, hh: (xx + 2, hh), "over" + name),
        ]
        return sum_blocks([mine, *got])

    one = ((n,), (n,))
    cut = n // 2
    tables = [place(one), place(((n,), (cut, cut))), dealt(), [(x % 2 == side) == (zh == y % 2)]]
    starts = [sum(len(t) for t in tables[:i]) for i in range(len(tables))]
    table = jnp.stack([jnp.asarray(v, jnp.int32) for t in tables for v in t])
    queries, table = lax.optimization_barrier((queries, table))

    own = condition(queries, left_inverse, right_inverse, 0, n)
    s0 = send(own, SAME, "s0")
    q0 = send(own, OPPOSITE, "q0")
    o1 = send(own, ACROSS, "o1")
    own_sib = send(own, SIBLING, "own_sib")
    stored = after(stored_rows, own).reshape(row_count, width)
    s0, q0, o1, stored = lax.optimization_barrier((s0, q0, o1, stored))
    t0 = send(q0, SAME, "t0")
    q1 = send(o1, OPPOSITE, "q1")
    s1 = send(s0, ACROSS, "s1")
    o1_sib, q0_sib, s0_sib = send(o1, SIBLING, "o1_sib"), send(q0, SIBLING, "q0_sib"), send(s0, SIBLING, "s0_sib")
    scores_o = score_group(table, starts[0], [own, o1, own_sib, o1_sib], stored)

    t0, q1, s1, scores_o = lax.optimization_barrier((t0, q1, s1, scores_o))
    first, second = split(q1, t0, cut)
    last = [send(first, SAME, "t1a"), send(second, ACROSS, "t1b")]
    q1_sib, s1_sib, t0_sib = send(q1, SIBLING, "q1_sib"), send(s1, SIBLING, "s1_sib"), send(t0, SIBLING, "t0_sib")
    dealt_1 = score_group(table, starts[0], [q0, q1, q0_sib, q1_sib], stored, scores_o, starts[2])
    *dealt_1, s1_sib, t0_sib = lax.optimization_barrier((*dealt_1, s1_sib, t0_sib))
    scores_s = score_group(table, starts[0], [after(s0, *dealt_1), s1, s0_sib, s1_sib], stored)
    last_sib = [send(after(piece, scores_s), SIBLING, "t1_sib") for piece in last]
    keep_1, onward_1 = reduce_batch(dealt_1, "_oq")
    dealt_2 = score_group(
        table, starts[1], [t0, *last, t0_sib, *last_sib], stored, scores_s, starts[2]
    )
    keep_2, onward_2 = reduce_batch(dealt_2, "_st")

    def final_first(yy, xx, hh):
        return (xx % 2 == yy // 2) == (hh == yy % 2)

    got_1 = whole(
        onward_1, lambda zz, yy, xx, hh: None if final_first(yy, xx, hh) else (xx, 1 - hh), "oq"
    )
    got_2 = whole(
        onward_2, lambda zz, yy, xx, hh: (xx, 1 - hh) if final_first(yy, xx, hh) else None, "st"
    )
    return finish(table, starts[3], [keep_2, keep_1], [got_2, got_1])


def solution(mesh):
    in_specs = (
        P("rows", "layers", None),
        P("rows", "layers", None),
        P("layers", None, None),
        P("layers", None, None),
    )
    out_specs = P("layers", "rows")
    return jax.shard_map(
        per_device, mesh=mesh, in_specs=in_specs, out_specs=out_specs, check_vma=False
    )
```

```python
import functools

import jax
import jax.numpy as jnp
from jax import lax
from jax.experimental import pallas as pl
from jax.experimental.pallas import tpu as pltpu
from jax.sharding import PartitionSpec as P

EPS = 1e-06
BF = jnp.bfloat16
F32 = jnp.float32
PAD = 128
MIB = 1 << 20

Z, Y, C, X, ZH = 2, 4, 2, 4, 2
BOTH = ("rows", "layers")


def rows_index(z, y, c):
    return (z * Y + y % Y) * C + c


def rows_perm(move):
    pairs = []
    for z in range(Z):
        for y in range(Y):
            for c in range(C):
                pairs.append((rows_index(z, y, c), rows_index(*move(z, y, c))))
    return pairs


SAME = rows_perm(lambda z, y, c: (z, y ^ 1, c))
OPPOSITE = rows_perm(lambda z, y, c: (z, y - 1 if y % 2 == 0 else y + 1, c))
ACROSS = rows_perm(lambda z, y, c: (1 - z, y, c))
SIBLING = rows_perm(lambda z, y, c: (z, y, 1 - c))


def whole_perm(move):
    pairs = []
    for z in range(Z):
        for y in range(Y):
            for c in range(C):
                for x in range(X):
                    for zh in range(ZH):
                        to = move(z, y, x, zh)
                        if to is not None:
                            r = rows_index(z, y, c)
                            source = r * X * ZH + x * ZH + zh
                            target = r * X * ZH + (to[0] % X) * ZH + to[1]
                            pairs.append((source, target))
    return pairs


def norm_columns(norms):
    count = norms.shape[0]
    high = norms.astype(BF).astype(F32)
    low = norms - high
    lane = lax.broadcasted_iota(jnp.int32, (count, PAD), 1)
    return jnp.where(lane < PAD // 2, high, low).astype(BF)


def thirds(value):
    parts = []
    for _ in range(3):
        parts.append(value.astype(BF))
        value = value - parts[-1].astype(F32)
    return parts

def dot(a, b):
    return lax.dot_general(a, b, (((1,), (0,)), ((), ())), preferred_element_type=F32)

def condition_kernel(q, left, right, out, swapped, back, turned_left):
    layers, count, width = q.shape
    side = right.shape[1]
    four = 4 * side
    tiles = width // 128
    row = lax.broadcasted_iota(jnp.int32, (four, four), 0)
    col = lax.broadcasted_iota(jnp.int32, (four, four), 1)
    right_mask = row // side == col // side
    left_mask = row % 128 // 32 == col % 128 // 32
    total = jnp.zeros((count, 128), F32)
    for l in range(layers):
        lanes = jnp.concatenate([right[l]] * 4, axis=1)
        wide_r = jnp.where(right_mask, jnp.concatenate([lanes] * 4, axis=0), 0.0)
        x = q[l]
        rows = jnp.concatenate([x[:, four * g : four * (g + 1)] for g in range(width // four)], axis=0)
        first = sum(dot(rows, part) for part in reversed(thirds(wide_r)))
        for g in range(width // four):
            for h in range(four // 128):
                swapped[g * (four // 128) + h] = first[count * g : count * (g + 1), 128 * h : 128 * (h + 1)]
        half = side // 2
        def halves(slot):
            return [turned_left[slot, pl.ds(i, half, stride=2), :] for i in range(2)]

        turned_left[0] = jnp.concatenate([left[l]] * 2, axis=1)
        low, high = halves(0)
        turn = jnp.concatenate([low] * 4 + [high] * 4, axis=0).T[:side]
        turned_left[1] = turn[:, :128]
        turned_left[2] = turn[:, 128:]
        low, high = (jnp.concatenate(pair, axis=1) for pair in zip(halves(1), halves(2)))
        wide_l = jnp.where(left_mask, jnp.concatenate([low] * 4 + [high] * 4, axis=0), 0.0)
        stack = []
        for j in range(count // 4):
            block = jnp.concatenate([swapped[:, 4 * j + i, :] for i in range(4)], axis=0).T
            stack.append(jnp.concatenate([block[:side], block[side:]], axis=1))
        turned = thirds(jnp.concatenate(stack, axis=0))
        factor = thirds(wide_l)
        second = dot(turned[1], factor[1]) + dot(turned[0], factor[2]) + dot(turned[2], factor[0])
        second = second + (dot(turned[0], factor[1]) + dot(turned[1], factor[0]))
        second = second + dot(turned[0], factor[0])
        for j in range(count // 4):
            piece = second[side * j : side * (j + 1)]
            block = jnp.concatenate([piece[:, :128], piece[:, 128:]], axis=0).T
            for i in range(4):
                back[4 * j + i] = block[32 * i : 32 * (i + 1)]
        for t in range(tiles):
            done = back[:, t, :].astype(BF)
            out[:, l * width + 128 * t : l * width + 128 * (t + 1)] = done
            wide = done.astype(F32)
            total = total + wide * wide
    out[:, layers * width :] = norm_columns(jnp.sum(total, axis=1, keepdims=True))

def condition(q, left, right):
    layers, count, width = q.shape
    side = left.shape[1]
    vmem = pl.BlockSpec(memory_space=pltpu.VMEM)
    return pl.pallas_call(
        condition_kernel,
        out_shape=jax.ShapeDtypeStruct((count, layers * width + PAD), BF),
        in_specs=[vmem] * 3,
        out_specs=vmem,
        scratch_shapes=[
            pltpu.VMEM((width // 128, count, 128), F32),
            pltpu.VMEM((count, width // 128, 128), F32),
            pltpu.VMEM((3, side, 128), F32),
        ],
        compiler_params=pltpu.CompilerParams(vmem_limit_bytes=24 * MIB),
        name="condition",
    )(q, left, right)


def fill(at, place, pieces, group):
    for i, piece in enumerate(pieces):
        rows = piece.shape[0]
        group[pl.ds(pl.multiple_of(place[at + i], 16), rows), :] = piece[...]


def products(group, stored):
    width = stored.shape[1]
    return lax.dot_general(
        group[:, :width], stored[...], (((1,), (1,)), ((), ())), preferred_element_type=F32
    )


def score_kernel(at, place, *refs):
    *pieces, stored, scores, group = refs
    edge = scores.shape[1] - PAD
    fill(at, place, pieces, group)
    scores[:, :edge] = products(group, stored).astype(BF)
    scores[:, edge:] = group[:, stored.shape[1] :]


def deal_kernel(at, deal, place, *refs):
    *pieces, stored, before, o0, o1, o2, o3, group, blocks = refs
    edge = before.shape[1] - PAD
    rows = before.shape[0]
    fill(at, place, pieces, group)
    blocks[:rows] = before[...]
    blocks[rows:, :edge] = products(group, stored).astype(BF)
    blocks[rows:, edge:] = group[:, stored.shape[1] :]
    for j, out in enumerate((o0, o1, o2, o3)):
        start = pl.multiple_of(place[deal + j] * out.shape[0], 128)
        out[...] = blocks[pl.ds(start, out.shape[0]), :]


def score_group(place, at, pieces, stored, before=None, deal=None):
    count, width = stored.shape
    rows = sum(p.shape[0] for p in pieces)
    vmem = pl.BlockSpec(memory_space=pltpu.VMEM)
    scratch = [pltpu.VMEM((rows, width + PAD), BF)]
    shape = jax.ShapeDtypeStruct((rows, count + PAD), BF)
    more = []
    if before is None:
        kernel, name = functools.partial(score_kernel, at), "score_group"
        out, out_specs = shape, vmem
    else:
        kernel, name = functools.partial(deal_kernel, at, deal), "score_and_deal"
        out = [jax.ShapeDtypeStruct((rows // 2, count + PAD), BF)] * 4
        out_specs = [vmem] * 4
        scratch.append(pltpu.VMEM((2 * rows, count + PAD), BF))
        more = [before]
    return pl.pallas_call(
        kernel,
        out_shape=out,
        in_specs=[pl.BlockSpec(memory_space=pltpu.SMEM)] + [vmem] * (len(pieces) + 1 + len(more)),
        out_specs=out_specs,
        scratch_shapes=scratch,
        compiler_params=pltpu.CompilerParams(vmem_limit_bytes=12 * MIB),
        cost_estimate=pl.CostEstimate(
            flops=2 * rows * width * count, bytes_accessed=2 * count * width, transcendentals=0
        ),
        name=name,
    )(place, *pieces, stored, *more)


def sum_kernel(v, a, b, c, keep, onward):
    edge = v.shape[1] - PAD
    total = v[...].astype(F32) + a[...].astype(F32) + b[...].astype(F32) + c[...].astype(F32)
    norms = total[:, edge : edge + 1] + total[:, edge + PAD // 2 : edge + PAD // 2 + 1]
    keep[:, :edge] = total[:, :edge]
    keep[:, edge:] = jnp.broadcast_to(norms, (v.shape[0], PAD))
    onward[:, :edge] = total[:, :edge].astype(BF)
    onward[:, edge:] = norm_columns(norms)


def sum_blocks(blocks):
    shape = blocks[0].shape
    vmem = pl.BlockSpec(memory_space=pltpu.VMEM)
    return pl.pallas_call(
        sum_kernel,
        out_shape=(jax.ShapeDtypeStruct(shape, F32), jax.ShapeDtypeStruct(shape, BF)),
        in_specs=[vmem] * 4,
        out_specs=(vmem, vmem),
        compiler_params=pltpu.CompilerParams(vmem_limit_bytes=6 * MIB),
        name="sum_blocks",
    )(*blocks)


def finish_kernel(at, which, keep_0, keep_1, got_0, got_1, out):
    edge = out.shape[1]

    def write(keep, got):
        more = got[...].astype(F32)
        norms = keep[:, edge : edge + 1] + (
            more[:, edge : edge + 1] + more[:, edge + PAD // 2 : edge + PAD // 2 + 1]
        )
        out[...] = (keep[:, :edge] + more[:, :edge]) * lax.rsqrt(norms + EPS)

    pl.when(which[at] == 0)(lambda: write(keep_0, got_0))
    pl.when(which[at] != 0)(lambda: write(keep_1, got_1))


def finish(which, at, keeps, gots):
    rows, width = keeps[0].shape
    vmem = pl.BlockSpec(memory_space=pltpu.VMEM)
    return pl.pallas_call(
        functools.partial(finish_kernel, at),
        out_shape=jax.ShapeDtypeStruct((rows, width - PAD), F32),
        in_specs=[pl.BlockSpec(memory_space=pltpu.SMEM)] + [vmem] * 4,
        out_specs=vmem,
        compiler_params=pltpu.CompilerParams(vmem_limit_bytes=4 * MIB),
        name="finish",
    )(which, *keeps, *gots)


def split_kernel(a, b, first, second):
    count = first.shape[0]
    first[...] = a[:count]
    second[...] = b[count:]


def split(a, b, count):
    vmem = pl.BlockSpec(memory_space=pltpu.VMEM)
    return pl.pallas_call(
        split_kernel,
        out_shape=[jax.ShapeDtypeStruct((size, a.shape[1]), a.dtype) for size in (count, b.shape[0] - count)],
        in_specs=[vmem] * 2,
        out_specs=[vmem] * 2,
        compiler_params=pltpu.CompilerParams(vmem_limit_bytes=4 * MIB),
        name="split",
    )(a, b)


def after(value, *others):
    return lax.optimization_barrier((value, *others))[0]


def per_device(queries, stored_rows, left_inverse, right_inverse):
    row_count = stored_rows.shape[0]
    width = stored_rows.shape[1] * stored_rows.shape[2]
    n = queries.shape[0]
    rows_at = lax.axis_index("rows")
    layers_at = lax.axis_index("layers")
    z, y, core = rows_at // (Y * C), (rows_at // C) % Y, rows_at % C
    x, zh = layers_at // ZH, layers_at % ZH
    side = y // 2

    def send(value, pairs, name):
        with jax.named_scope(name):
            return lax.ppermute(value, "rows", pairs)

    def whole(value, move, name):
        with jax.named_scope(name):
            return lax.ppermute(value, BOTH, whole_perm(move))

    def place(rows_of):
        offsets = []
        for at in (core, 1 - core):
            for block, rows in enumerate(rows_of):
                start = 2 * n * block + n * at
                for count in rows:
                    offsets.append(start)
                    start = start + count
        return offsets

    def dealt():
        to = [(x + step) % X for step in (0, 1, 2, 3)]
        return [2 * (t % 2 != side) + (t // 2 != z) for t in to]

    def reduce_batch(blocks, name):
        mine, up, over, down = blocks
        got = [
            whole(up, lambda zz, yy, xx, hh: (xx + 1, hh), "up" + name),
            whole(down, lambda zz, yy, xx, hh: (xx - 1, hh), "down" + name),
            whole(over, lambda zz, yy, xx, hh: (xx + 2, hh), "over" + name),
        ]
        return mine, *got

    one = ((n,), (n,))
    cut = n // 2
    tables = [place(one), dealt(), place(((n,), (cut, cut))), [(x % 2 == side) == (zh == y % 2)]]
    starts = [sum(len(t) for t in tables[:i]) for i in range(len(tables))]
    table = jnp.stack([jnp.asarray(v, jnp.int32) for t in tables for v in t])
    queries, table = lax.optimization_barrier((queries, table))

    own = condition(jnp.swapaxes(queries, 0, 1), left_inverse, right_inverse)
    s0 = send(own, SAME, "s0")
    q0 = send(own, OPPOSITE, "q0")
    o1 = send(own, ACROSS, "o1")
    own_sib = send(own, SIBLING, "own_sib")
    stored = after(stored_rows, own).reshape(row_count, width)
    s0, q0, o1, stored = lax.optimization_barrier((s0, q0, o1, stored))
    t0 = send(q0, SAME, "t0")
    q1 = send(o1, OPPOSITE, "q1")
    s1 = send(s0, ACROSS, "s1")
    o1_sib, q0_sib, s0_sib = send(o1, SIBLING, "o1_sib"), send(q0, SIBLING, "q0_sib"), send(s0, SIBLING, "s0_sib")
    scores_o = score_group(table, starts[0], [own, o1, own_sib, o1_sib], stored)

    t0, q1, s1, scores_o, s0_sib = lax.optimization_barrier((t0, q1, s1, scores_o, s0_sib))
    first, second = split(q1, t0, cut)
    t1a, t1b = send(first, SAME, "t1a"), send(second, ACROSS, "t1b")
    q1_sib, s1_sib, t0_sib = send(q1, SIBLING, "q1_sib"), send(s1, SIBLING, "s1_sib"), send(t0, SIBLING, "t0_sib")
    dealt_1 = score_group(table, starts[0], [q0, q1, q0_sib, q1_sib], stored, scores_o, starts[1])
    *dealt_1, s1_sib, t0_sib = lax.optimization_barrier((*dealt_1, s1_sib, t0_sib))
    mine, up, down, over = reduce_batch(dealt_1, "_oq")
    scores_s = score_group(table, starts[0], [after(s0, *dealt_1), s1, s0_sib, s1_sib], stored)
    t1a, t1b, scores_s, up, down = lax.optimization_barrier((t1a, t1b, scores_s, up, down))
    t1a_sib, t1b_sib = send(t1a, SIBLING, "t1a_sib"), send(t1b, SIBLING, "t1b_sib")
    keep_1, onward_1 = sum_blocks([mine, up, down, over])
    last = [t0, t1a, t1b, t0_sib, t1a_sib, t1b_sib]
    dealt_2 = score_group(table, starts[2], last, stored, scores_s, starts[1])
    keep_2, onward_2 = sum_blocks(reduce_batch(dealt_2, "_st"))

    def final_first(yy, xx, hh):
        return (xx % 2 == yy // 2) == (hh == yy % 2)

    got_1 = whole(
        onward_1, lambda zz, yy, xx, hh: None if final_first(yy, xx, hh) else (xx, 1 - hh), "oq"
    )
    got_2 = whole(
        onward_2, lambda zz, yy, xx, hh: (xx, 1 - hh) if final_first(yy, xx, hh) else None, "st"
    )
    return finish(table, starts[3], [keep_2, keep_1], [got_2, got_1])


def solution(mesh):
    in_specs = (
        P("rows", "layers", None),
        P("rows", "layers", None),
        P("layers", None, None),
        P("layers", None, None),
    )
    out_specs = P("layers", "rows")
    return jax.shard_map(
        per_device, mesh=mesh, in_specs=in_specs, out_specs=out_specs, check_vma=False
    )
```

```python
import functools

import jax
import jax.numpy as jnp
from jax import lax
from jax.experimental import pallas as pl
from jax.experimental.pallas import tpu as pltpu
from jax.sharding import PartitionSpec as P

EPS = 1e-06
BF = jnp.bfloat16
F32 = jnp.float32
PAD = 128
MIB = 1 << 20

Z, Y, C, X, ZH = 2, 4, 2, 4, 2
BOTH = ("rows", "layers")


def rows_index(z, y, c):
    return (z * Y + y % Y) * C + c


def rows_perm(move):
    pairs = []
    for z in range(Z):
        for y in range(Y):
            for c in range(C):
                pairs.append((rows_index(z, y, c), rows_index(*move(z, y, c))))
    return pairs


SAME = rows_perm(lambda z, y, c: (z, y ^ 1, c))
OPPOSITE = rows_perm(lambda z, y, c: (z, y - 1 if y % 2 == 0 else y + 1, c))
ACROSS = rows_perm(lambda z, y, c: (1 - z, y, c))
SIBLING = rows_perm(lambda z, y, c: (z, y, 1 - c))


def whole_perm(move):
    pairs = []
    for z in range(Z):
        for y in range(Y):
            for c in range(C):
                for x in range(X):
                    for zh in range(ZH):
                        to = move(z, y, x, zh)
                        if to is not None:
                            r = rows_index(z, y, c)
                            source = r * X * ZH + x * ZH + zh
                            target = r * X * ZH + (to[0] % X) * ZH + to[1]
                            pairs.append((source, target))
    return pairs


def norm_columns(norms):
    count = norms.shape[0]
    high = norms.astype(BF).astype(F32)
    low = norms - high
    lane = lax.broadcasted_iota(jnp.int32, (count, PAD), 1)
    return jnp.where(lane < PAD // 2, high, low).astype(BF)


def thirds(value):
    parts = []
    for _ in range(3):
        parts.append(value.astype(BF))
        value = value - parts[-1].astype(F32)
    return parts

def dot(a, b):
    return lax.dot_general(a, b, (((1,), (0,)), ((), ())), preferred_element_type=F32)

def condition_kernel(q, left, right, out, swapped, back, turned_left):
    layers, count, width = q.shape
    side = right.shape[1]
    four = 4 * side
    tiles = width // 128
    row = lax.broadcasted_iota(jnp.int32, (four, four), 0)
    col = lax.broadcasted_iota(jnp.int32, (four, four), 1)
    right_mask = row // side == col // side
    left_mask = row % 128 // 32 == col % 128 // 32
    total = jnp.zeros((count, 128), F32)
    for l in range(layers):
        lanes = jnp.concatenate([right[l]] * 4, axis=1)
        wide_r = jnp.where(right_mask, jnp.concatenate([lanes] * 4, axis=0), 0.0)
        x = q[l]
        rows = jnp.concatenate([x[:, four * g : four * (g + 1)] for g in range(width // four)], axis=0)
        first = sum(dot(rows, part) for part in reversed(thirds(wide_r)))
        for g in range(width // four):
            for h in range(four // 128):
                swapped[g * (four // 128) + h] = first[count * g : count * (g + 1), 128 * h : 128 * (h + 1)]
        half = side // 2
        def halves(slot):
            return [turned_left[slot, pl.ds(i, half, stride=2), :] for i in range(2)]

        turned_left[0] = jnp.concatenate([left[l]] * 2, axis=1)
        low, high = halves(0)
        turn = jnp.concatenate([low] * 4 + [high] * 4, axis=0).T[:side]
        turned_left[1] = turn[:, :128]
        turned_left[2] = turn[:, 128:]
        low, high = (jnp.concatenate(pair, axis=1) for pair in zip(halves(1), halves(2)))
        wide_l = jnp.where(left_mask, jnp.concatenate([low] * 4 + [high] * 4, axis=0), 0.0)
        stack = []
        for j in range(count // 4):
            block = jnp.concatenate([swapped[:, 4 * j + i, :] for i in range(4)], axis=0).T
            stack.append(jnp.concatenate([block[:side], block[side:]], axis=1))
        turned = thirds(jnp.concatenate(stack, axis=0))
        factor = thirds(wide_l)
        second = dot(turned[1], factor[1]) + dot(turned[0], factor[2]) + dot(turned[2], factor[0])
        second = second + (dot(turned[0], factor[1]) + dot(turned[1], factor[0]))
        second = second + dot(turned[0], factor[0])
        for j in range(count // 4):
            piece = second[side * j : side * (j + 1)]
            block = jnp.concatenate([piece[:, :128], piece[:, 128:]], axis=0).T
            for i in range(4):
                back[4 * j + i] = block[32 * i : 32 * (i + 1)]
        for t in range(tiles):
            done = back[:, t, :].astype(BF)
            out[:, l * width + 128 * t : l * width + 128 * (t + 1)] = done
            wide = done.astype(F32)
            total = total + wide * wide
    out[:, layers * width :] = norm_columns(jnp.sum(total, axis=1, keepdims=True))

def condition(q, left, right):
    layers, count, width = q.shape
    side = left.shape[1]
    vmem = pl.BlockSpec(memory_space=pltpu.VMEM)
    return pl.pallas_call(
        condition_kernel,
        out_shape=jax.ShapeDtypeStruct((count, layers * width + PAD), BF),
        in_specs=[vmem] * 3,
        out_specs=vmem,
        scratch_shapes=[
            pltpu.VMEM((width // 128, count, 128), F32),
            pltpu.VMEM((count, width // 128, 128), F32),
            pltpu.VMEM((3, side, 128), F32),
        ],
        compiler_params=pltpu.CompilerParams(vmem_limit_bytes=24 * MIB),
        name="condition",
    )(q, left, right)


def fill(at, place, pieces, group):
    for i, piece in enumerate(pieces):
        rows = piece.shape[0]
        group[pl.ds(pl.multiple_of(place[at + i], 16), rows), :] = piece[...]


def products(group, stored):
    width = stored.shape[1]
    return lax.dot_general(
        group[:, :width], stored[...], (((1,), (1,)), ((), ())), preferred_element_type=F32
    )


def score_kernel(at, place, *refs):
    *pieces, stored, scores, group = refs
    edge = scores.shape[1] - PAD
    fill(at, place, pieces, group)
    scores[:, :edge] = products(group, stored).astype(BF)
    scores[:, edge:] = group[:, stored.shape[1] :]


def deal_kernel(at, deal, parts, count, place, *refs):
    pieces, stored, before = refs[:count], refs[count], refs[count + 1]
    outs, (group, blocks) = refs[count + 2 : -2], refs[-2:]
    edge = before.shape[1] - PAD
    rows = before.shape[0]
    fill(at, place, pieces, group)
    blocks[:rows] = before[...]
    blocks[rows:, :edge] = products(group, stored).astype(BF)
    blocks[rows:, edge:] = group[:, stored.shape[1] :]
    size = rows // 2
    for j in range(4):
        take = pl.ds(pl.multiple_of(place[deal + j] * size, 128), size)
        if parts == 1:
            outs[j][...] = blocks[take, :]
        else:
            first, second = outs[2 * j], outs[2 * j + 1]
            cut = second.shape[1]
            first[:, :cut] = blocks[take, :cut]
            first[:, cut:] = blocks[take, edge:]
            second[...] = blocks[take, cut:edge]


def score_group(place, at, pieces, stored, before=None, deal=None, parts=1):
    count, width = stored.shape
    rows = sum(p.shape[0] for p in pieces)
    vmem = pl.BlockSpec(memory_space=pltpu.VMEM)
    scratch = [pltpu.VMEM((rows, width + PAD), BF)]
    shape = jax.ShapeDtypeStruct((rows, count + PAD), BF)
    more = []
    if before is None:
        kernel, name = functools.partial(score_kernel, at), "score_group"
        out, out_specs = shape, vmem
    else:
        kernel, name = functools.partial(deal_kernel, at, deal, parts, len(pieces)), "score_and_deal"
        widths = [count + PAD] if parts == 1 else [count // 2 + PAD, count // 2]
        out = [jax.ShapeDtypeStruct((rows // 2, w), BF) for w in widths] * 4
        out_specs = [vmem] * len(out)
        scratch.append(pltpu.VMEM((2 * rows, count + PAD), BF))
        more = [before]
    return pl.pallas_call(
        kernel,
        out_shape=out,
        in_specs=[pl.BlockSpec(memory_space=pltpu.SMEM)] + [vmem] * (len(pieces) + 1 + len(more)),
        out_specs=out_specs,
        scratch_shapes=scratch,
        compiler_params=pltpu.CompilerParams(vmem_limit_bytes=12 * MIB),
        cost_estimate=pl.CostEstimate(
            flops=2 * rows * width * count, bytes_accessed=2 * count * width, transcendentals=0
        ),
        name=name,
    )(place, *pieces, stored, *more)


def sum_kernel(v, a, b, c, keep, onward):
    edge = v.shape[1] - PAD
    total = v[...].astype(F32) + a[...].astype(F32) + b[...].astype(F32) + c[...].astype(F32)
    norms = total[:, edge : edge + 1] + total[:, edge + PAD // 2 : edge + PAD // 2 + 1]
    keep[:, :edge] = total[:, :edge]
    keep[:, edge:] = jnp.broadcast_to(norms, (v.shape[0], PAD))
    onward[:, :edge] = total[:, :edge].astype(BF)
    onward[:, edge:] = norm_columns(norms)


def plain_kernel(v, a, b, c, keep, onward):
    total = v[...].astype(F32) + a[...].astype(F32) + b[...].astype(F32) + c[...].astype(F32)
    keep[...] = total
    onward[...] = total.astype(BF)


def sum_blocks(blocks, with_norms=True):
    shape = blocks[0].shape
    vmem = pl.BlockSpec(memory_space=pltpu.VMEM)
    return pl.pallas_call(
        sum_kernel if with_norms else plain_kernel,
        out_shape=(jax.ShapeDtypeStruct(shape, F32), jax.ShapeDtypeStruct(shape, BF)),
        in_specs=[vmem] * 4,
        out_specs=(vmem, vmem),
        compiler_params=pltpu.CompilerParams(vmem_limit_bytes=6 * MIB),
        name="sum_blocks",
    )(*blocks)


def finish_kernel(at, which, *refs):
    *parts, out = refs

    def scale(keep, got):
        edge = keep.shape[1] - PAD
        more = got[:, edge:].astype(F32)
        norms = keep[:, edge : edge + 1] + (more[:, :1] + more[:, PAD // 2 : PAD // 2 + 1])
        return lax.rsqrt(norms + EPS)

    def write(pairs):
        by = scale(*pairs[0])
        start = 0
        for i, (keep, got) in enumerate(pairs):
            stop = start + keep.shape[1] - (PAD if i == 0 else 0)
            out[:, start:stop] = (keep[:, : stop - start] + got[:, : stop - start].astype(F32)) * by
            start = stop

    pl.when(which[at] == 0)(lambda: write([parts[0:2], parts[2:4]]))
    pl.when(which[at] != 0)(lambda: write([parts[4:6]]))


def finish(which, at, late, early, columns):
    vmem = pl.BlockSpec(memory_space=pltpu.VMEM)
    arrays = [array for pair in (*late, *early) for array in pair]
    return pl.pallas_call(
        functools.partial(finish_kernel, at),
        out_shape=jax.ShapeDtypeStruct((arrays[0].shape[0], columns), F32),
        in_specs=[pl.BlockSpec(memory_space=pltpu.SMEM)] + [vmem] * len(arrays),
        out_specs=vmem,
        compiler_params=pltpu.CompilerParams(vmem_limit_bytes=4 * MIB),
        name="finish",
    )(which, *arrays)


def split_kernel(a, b, first, second):
    count = first.shape[0]
    first[...] = a[:count]
    second[...] = b[count:]


def split(a, b, count):
    vmem = pl.BlockSpec(memory_space=pltpu.VMEM)
    return pl.pallas_call(
        split_kernel,
        out_shape=[jax.ShapeDtypeStruct((size, a.shape[1]), a.dtype) for size in (count, b.shape[0] - count)],
        in_specs=[vmem] * 2,
        out_specs=[vmem] * 2,
        compiler_params=pltpu.CompilerParams(vmem_limit_bytes=4 * MIB),
        name="split",
    )(a, b)


def after(value, *others):
    return lax.optimization_barrier((value, *others))[0]


def per_device(queries, stored_rows, left_inverse, right_inverse):
    row_count = stored_rows.shape[0]
    width = stored_rows.shape[1] * stored_rows.shape[2]
    n = queries.shape[0]
    rows_at = lax.axis_index("rows")
    layers_at = lax.axis_index("layers")
    z, y, core = rows_at // (Y * C), (rows_at // C) % Y, rows_at % C
    x, zh = layers_at // ZH, layers_at % ZH
    side = y // 2

    def send(value, pairs, name):
        with jax.named_scope(name):
            return lax.ppermute(value, "rows", pairs)

    def whole(value, move, name):
        with jax.named_scope(name):
            return lax.ppermute(value, BOTH, whole_perm(move))

    def place(rows_of):
        offsets = []
        for at in (core, 1 - core):
            for block, rows in enumerate(rows_of):
                start = 2 * n * block + n * at
                for count in rows:
                    offsets.append(start)
                    start = start + count
        return offsets

    def dealt():
        to = [(x + step) % X for step in (0, 1, 2, 3)]
        return [2 * (t % 2 != side) + (t // 2 != z) for t in to]

    def reduce_batch(blocks, name):
        mine, up, over, down = blocks
        got = [
            whole(up, lambda zz, yy, xx, hh: (xx + 1, hh), "up" + name),
            whole(down, lambda zz, yy, xx, hh: (xx - 1, hh), "down" + name),
            whole(over, lambda zz, yy, xx, hh: (xx + 2, hh), "over" + name),
        ]
        return mine, *got

    one = ((n,), (n,))
    cut = n // 2
    tables = [place(one), dealt(), place(((n,), (cut, cut))), [(x % 2 == side) == (zh == y % 2)]]
    starts = [sum(len(t) for t in tables[:i]) for i in range(len(tables))]
    table = jnp.stack([jnp.asarray(v, jnp.int32) for t in tables for v in t])
    queries, table = lax.optimization_barrier((queries, table))

    own = condition(jnp.swapaxes(queries, 0, 1), left_inverse, right_inverse)
    s0 = send(own, SAME, "s0")
    q0 = send(own, OPPOSITE, "q0")
    o1 = send(own, ACROSS, "o1")
    own_sib = send(own, SIBLING, "own_sib")
    stored = after(stored_rows, own).reshape(row_count, width)
    s0, q0, o1, stored = lax.optimization_barrier((s0, q0, o1, stored))
    t0 = send(q0, SAME, "t0")
    q1 = send(o1, OPPOSITE, "q1")
    s1 = send(s0, ACROSS, "s1")
    o1_sib, q0_sib, s0_sib = send(o1, SIBLING, "o1_sib"), send(q0, SIBLING, "q0_sib"), send(s0, SIBLING, "s0_sib")
    scores_o = score_group(table, starts[0], [own, o1, own_sib, o1_sib], stored)

    t0, q1, s1, scores_o, s0_sib = lax.optimization_barrier((t0, q1, s1, scores_o, s0_sib))
    first, second = split(q1, t0, cut)
    t1a, t1b = send(first, SAME, "t1a"), send(second, ACROSS, "t1b")
    q1_sib, s1_sib, t0_sib = send(q1, SIBLING, "q1_sib"), send(s1, SIBLING, "s1_sib"), send(t0, SIBLING, "t0_sib")
    dealt_1 = score_group(table, starts[0], [q0, q1, q0_sib, q1_sib], stored, scores_o, starts[1])
    *dealt_1, s1_sib, t0_sib = lax.optimization_barrier((*dealt_1, s1_sib, t0_sib))
    mine, up, down, over = reduce_batch(dealt_1, "_oq")
    scores_s = score_group(table, starts[0], [after(s0, *dealt_1), s1, s0_sib, s1_sib], stored)
    t1a, t1b, scores_s, up, down = lax.optimization_barrier((t1a, t1b, scores_s, up, down))
    t1a_sib, t1b_sib = send(t1a, SIBLING, "t1a_sib"), send(t1b, SIBLING, "t1b_sib")
    keep_1, onward_1 = sum_blocks([mine, up, down, over])
    last = [t0, t1a, t1b, t0_sib, t1a_sib, t1b_sib]
    dealt_2 = score_group(
        table, starts[2], last, stored, scores_s, starts[1], parts=2
    )
    keep_2, onward_2 = sum_blocks(reduce_batch(dealt_2[0::2], "_st"))
    keep_3, onward_3 = sum_blocks(reduce_batch(dealt_2[1::2], "_st_right"), with_norms=False)

    def final_first(yy, xx, hh):
        return (xx % 2 == yy // 2) == (hh == yy % 2)

    def other(zz, yy, xx, hh):
        return (xx, 1 - hh) if final_first(yy, xx, hh) else None

    got_1 = whole(
        onward_1, lambda zz, yy, xx, hh: None if final_first(yy, xx, hh) else (xx, 1 - hh), "oq"
    )
    got_2 = whole(onward_2, other, "st")
    got_3 = whole(onward_3, other, "st_right")
    late = [(keep_2, got_2), (keep_3, got_3)]
    return finish(table, starts[3], late, [(keep_1, got_1)], row_count)


def solution(mesh):
    in_specs = (
        P("rows", "layers", None),
        P("rows", "layers", None),
        P("layers", None, None),
        P("layers", None, None),
    )
    out_specs = P("layers", "rows")
    return jax.shard_map(
        per_device, mesh=mesh, in_specs=in_specs, out_specs=out_specs, check_vma=False
    )
```

```python
import functools

import jax
import jax.numpy as jnp
from jax import lax
from jax.experimental import pallas as pl
from jax.experimental.pallas import tpu as pltpu
from jax.sharding import PartitionSpec as P

EPS = 1e-06
BF = jnp.bfloat16
F32 = jnp.float32
PAD = 128
MIB = 1 << 20

Z, Y, C, X, ZH = 2, 4, 2, 4, 2
BOTH = ("rows", "layers")


def rows_index(z, y, c):
    return (z * Y + y % Y) * C + c


def rows_perm(move):
    pairs = []
    for z in range(Z):
        for y in range(Y):
            for c in range(C):
                pairs.append((rows_index(z, y, c), rows_index(*move(z, y, c))))
    return pairs


SAME = rows_perm(lambda z, y, c: (z, y ^ 1, c))
OPPOSITE = rows_perm(lambda z, y, c: (z, y - 1 if y % 2 == 0 else y + 1, c))
ACROSS = rows_perm(lambda z, y, c: (1 - z, y, c))
SIBLING = rows_perm(lambda z, y, c: (z, y, 1 - c))


def whole_perm(move):
    pairs = []
    for z in range(Z):
        for y in range(Y):
            for c in range(C):
                for x in range(X):
                    for zh in range(ZH):
                        to = move(z, y, x, zh)
                        if to is not None:
                            r = rows_index(z, y, c)
                            source = r * X * ZH + x * ZH + zh
                            target = r * X * ZH + (to[0] % X) * ZH + to[1]
                            pairs.append((source, target))
    return pairs


def norm_columns(norms):
    count = norms.shape[0]
    high = norms.astype(BF).astype(F32)
    low = norms - high
    lane = lax.broadcasted_iota(jnp.int32, (count, PAD), 1)
    return jnp.where(lane < PAD // 2, high, low).astype(BF)


def thirds(value):
    parts = []
    for _ in range(3):
        parts.append(value.astype(BF))
        value = value - parts[-1].astype(F32)
    return parts


def dot(a, b):
    return lax.dot_general(a, b, (((1,), (0,)), ((), ())), preferred_element_type=F32)


def condition_kernel(q, left, right, out, back, turned_left):
    count, layers = out.shape[0], q.shape[0]
    width = q.shape[1] * q.shape[2] // count
    side = right.shape[1]
    four = 4 * side
    tiles = width // 128
    row = lax.broadcasted_iota(jnp.int32, (four, four), 0)
    col = lax.broadcasted_iota(jnp.int32, (four, four), 1)
    right_mask = row // side == col // side
    left_mask = row % 128 // 32 == col % 128 // 32
    total = jnp.zeros((count, 128), F32)
    for l in range(layers):
        lanes = jnp.concatenate([right[l]] * 4, axis=1)
        wide_r = jnp.where(right_mask, jnp.concatenate([lanes] * 4, axis=0), 0.0)
        once = sum(dot(q[l], part) for part in reversed(thirds(wide_r)))
        quarter = side // 4

        def spread(slot, order):
            return [turned_left[slot, pl.ds(i, quarter, stride=4), :] for i in order]

        turned_left[0] = jnp.concatenate([left[l]] * 2, axis=1)
        low, high = (turned_left[0, pl.ds(i, side // 2, stride=2), :] for i in range(2))
        turn = jnp.concatenate([low] * 4 + [high] * 4, axis=0).T[:side]
        turned_left[1] = turn[:, :128]
        turned_left[2] = turn[:, 128:]
        rows = [jnp.concatenate(p, axis=1) for p in zip(spread(1, (0, 2, 1, 3)), spread(2, (0, 2, 1, 3)))]
        low, high = jnp.concatenate(rows[:2], axis=0), jnp.concatenate(rows[2:], axis=0)
        wide_l = jnp.where(left_mask, jnp.concatenate([low] * 4 + [high] * 4, axis=0), 0.0)
        stack = []
        groups = width // four
        for j in range(count // 4):
            pieces = []
            for i in range(4):
                mine = once[groups * (4 * j + i) : groups * (4 * j + i + 1)]
                pieces += [mine[:, :128], mine[:, 128:]]
            block = jnp.concatenate(pieces, axis=0).T
            stack.append(jnp.concatenate([block[:side], block[side:]], axis=1))
        turned = thirds(jnp.concatenate(stack, axis=0))
        factor = thirds(wide_l)
        second = dot(turned[1], factor[1]) + dot(turned[0], factor[2]) + dot(turned[2], factor[0])
        second = second + (dot(turned[0], factor[1]) + dot(turned[1], factor[0]))
        second = second + dot(turned[0], factor[0])
        for j in range(count // 4):
            piece = second[side * j : side * (j + 1)]
            block = jnp.concatenate([piece[:, :128], piece[:, 128:]], axis=0).T
            for i in range(4):
                back[4 * j + i] = block[32 * i : 32 * (i + 1)]
        for t in range(tiles):
            done = back[:, t, :].astype(BF)
            out[:, l * width + 128 * t : l * width + 128 * (t + 1)] = done
            wide = done.astype(F32)
            total = total + wide * wide
    out[:, layers * width :] = norm_columns(jnp.sum(total, axis=1, keepdims=True))


def condition(queries, left, right):
    count, layers, width = queries.shape
    side = left.shape[1]
    four = 4 * side
    q = jnp.transpose(queries.reshape(count, layers, width // four, four), (1, 0, 2, 3))
    vmem = pl.BlockSpec(memory_space=pltpu.VMEM)
    return pl.pallas_call(
        condition_kernel,
        out_shape=jax.ShapeDtypeStruct((count, layers * width + PAD), BF),
        in_specs=[vmem] * 3,
        out_specs=vmem,
        scratch_shapes=[
            pltpu.VMEM((count, width // 128, 128), F32),
            pltpu.VMEM((3, side, 128), F32),
        ],
        compiler_params=pltpu.CompilerParams(vmem_limit_bytes=24 * MIB),
        name="condition",
    )(q.reshape(layers, count * width // four, four), left, right)


def fill(at, place, pieces, group):
    for i, piece in enumerate(pieces):
        rows = piece.shape[0]
        group[pl.ds(pl.multiple_of(place[at + i], 16), rows), :] = piece[...]


def products(group, stored):
    width = stored.shape[1]
    return lax.dot_general(
        group[:, :width], stored[...], (((1,), (1,)), ((), ())), preferred_element_type=F32
    )


def score_kernel(at, place, *refs):
    *pieces, stored, scores, group = refs
    edge = scores.shape[1] - PAD
    fill(at, place, pieces, group)
    scores[:, :edge] = products(group, stored).astype(BF)
    scores[:, edge:] = group[:, stored.shape[1] :]


def deal_kernel(at, deal, parts, count, place, *refs):
    pieces, stored, before = refs[:count], refs[count], refs[count + 1]
    outs, (group, blocks) = refs[count + 2 : -2], refs[-2:]
    edge = before.shape[1] - PAD
    rows = before.shape[0]
    fill(at, place, pieces, group)
    blocks[:rows] = before[...]
    blocks[rows:, :edge] = products(group, stored).astype(BF)
    blocks[rows:, edge:] = group[:, stored.shape[1] :]
    size = rows // 2
    for j in range(4):
        take = pl.ds(pl.multiple_of(place[deal + j] * size, 128), size)
        if parts == 1:
            outs[j][...] = blocks[take, :]
        else:
            first, second = outs[2 * j], outs[2 * j + 1]
            cut = second.shape[1]
            first[:, :cut] = blocks[take, :cut]
            first[:, cut:] = blocks[take, edge:]
            second[...] = blocks[take, cut:edge]


def score_group(place, at, pieces, stored, before=None, deal=None, parts=1):
    count, width = stored.shape
    rows = sum(p.shape[0] for p in pieces)
    vmem = pl.BlockSpec(memory_space=pltpu.VMEM)
    scratch = [pltpu.VMEM((rows, width + PAD), BF)]
    shape = jax.ShapeDtypeStruct((rows, count + PAD), BF)
    more = []
    if before is None:
        kernel, name = functools.partial(score_kernel, at), "score_group"
        out, out_specs = shape, vmem
    else:
        kernel, name = functools.partial(deal_kernel, at, deal, parts, len(pieces)), "score_and_deal"
        widths = [count + PAD] if parts == 1 else [count // 2 + PAD, count // 2]
        out = [jax.ShapeDtypeStruct((rows // 2, w), BF) for w in widths] * 4
        out_specs = [vmem] * len(out)
        scratch.append(pltpu.VMEM((2 * rows, count + PAD), BF))
        more = [before]
    return pl.pallas_call(
        kernel,
        out_shape=out,
        in_specs=[pl.BlockSpec(memory_space=pltpu.SMEM)] + [vmem] * (len(pieces) + 1 + len(more)),
        out_specs=out_specs,
        scratch_shapes=scratch,
        compiler_params=pltpu.CompilerParams(vmem_limit_bytes=12 * MIB),
        cost_estimate=pl.CostEstimate(
            flops=2 * rows * width * count, bytes_accessed=2 * count * width, transcendentals=0
        ),
        name=name,
    )(place, *pieces, stored, *more)


def sum_kernel(v, a, b, c, keep, onward):
    edge = v.shape[1] - PAD
    total = v[...].astype(F32) + a[...].astype(F32) + b[...].astype(F32) + c[...].astype(F32)
    norms = total[:, edge : edge + 1] + total[:, edge + PAD // 2 : edge + PAD // 2 + 1]
    keep[:, :edge] = total[:, :edge]
    keep[:, edge:] = jnp.broadcast_to(norms, (v.shape[0], PAD))
    onward[:, :edge] = total[:, :edge].astype(BF)
    onward[:, edge:] = norm_columns(norms)


def plain_kernel(v, a, b, c, keep, onward):
    total = v[...].astype(F32) + a[...].astype(F32) + b[...].astype(F32) + c[...].astype(F32)
    keep[...] = total
    onward[...] = total.astype(BF)


def sum_blocks(blocks, with_norms=True):
    shape = blocks[0].shape
    vmem = pl.BlockSpec(memory_space=pltpu.VMEM)
    return pl.pallas_call(
        sum_kernel if with_norms else plain_kernel,
        out_shape=(jax.ShapeDtypeStruct(shape, F32), jax.ShapeDtypeStruct(shape, BF)),
        in_specs=[vmem] * 4,
        out_specs=(vmem, vmem),
        compiler_params=pltpu.CompilerParams(vmem_limit_bytes=6 * MIB),
        name="sum_blocks",
    )(*blocks)


def finish_kernel(at, which, *refs):
    *parts, out = refs

    def scale(keep, got):
        edge = keep.shape[1] - PAD
        more = got[:, edge:].astype(F32)
        norms = keep[:, edge : edge + 1] + (more[:, :1] + more[:, PAD // 2 : PAD // 2 + 1])
        return lax.rsqrt(norms + EPS)

    def write(pairs):
        by = scale(*pairs[0])
        start = 0
        for i, (keep, got) in enumerate(pairs):
            stop = start + keep.shape[1] - (PAD if i == 0 else 0)
            out[:, start:stop] = (keep[:, : stop - start] + got[:, : stop - start].astype(F32)) * by
            start = stop

    pl.when(which[at] == 0)(lambda: write([parts[0:2], parts[2:4]]))
    pl.when(which[at] != 0)(lambda: write([parts[4:6]]))


def finish(which, at, late, early, columns):
    vmem = pl.BlockSpec(memory_space=pltpu.VMEM)
    arrays = [array for pair in (*late, *early) for array in pair]
    return pl.pallas_call(
        functools.partial(finish_kernel, at),
        out_shape=jax.ShapeDtypeStruct((arrays[0].shape[0], columns), F32),
        in_specs=[pl.BlockSpec(memory_space=pltpu.SMEM)] + [vmem] * len(arrays),
        out_specs=vmem,
        compiler_params=pltpu.CompilerParams(vmem_limit_bytes=4 * MIB),
        name="finish",
    )(which, *arrays)


def split_kernel(a, b, first, second):
    count = first.shape[0]
    first[...] = a[:count]
    second[...] = b[count:]


def split(a, b, count):
    vmem = pl.BlockSpec(memory_space=pltpu.VMEM)
    return pl.pallas_call(
        split_kernel,
        out_shape=[jax.ShapeDtypeStruct((size, a.shape[1]), a.dtype) for size in (count, b.shape[0] - count)],
        in_specs=[vmem] * 2,
        out_specs=[vmem] * 2,
        compiler_params=pltpu.CompilerParams(vmem_limit_bytes=4 * MIB),
        name="split",
    )(a, b)


def after(value, *others):
    return lax.optimization_barrier((value, *others))[0]


def per_device(queries, stored_rows, left_inverse, right_inverse):
    row_count = stored_rows.shape[0]
    width = stored_rows.shape[1] * stored_rows.shape[2]
    n = queries.shape[0]
    rows_at = lax.axis_index("rows")
    layers_at = lax.axis_index("layers")
    z, y, core = rows_at // (Y * C), (rows_at // C) % Y, rows_at % C
    x, zh = layers_at // ZH, layers_at % ZH
    side = y // 2

    def send(value, pairs, name):
        with jax.named_scope(name):
            return lax.ppermute(value, "rows", pairs)

    def whole(value, move, name):
        with jax.named_scope(name):
            return lax.ppermute(value, BOTH, whole_perm(move))

    def place(rows_of):
        offsets = []
        for at in (core, 1 - core):
            for block, rows in enumerate(rows_of):
                start = 2 * n * block + n * at
                for count in rows:
                    offsets.append(start)
                    start = start + count
        return offsets

    def dealt():
        to = [(x + step) % X for step in (0, 1, 2, 3)]
        return [2 * (t % 2 != side) + (t // 2 != z) for t in to]

    def reduce_batch(blocks, name):
        mine, up, over, down = blocks
        got = [
            whole(up, lambda zz, yy, xx, hh: (xx + 1, hh), "up" + name),
            whole(down, lambda zz, yy, xx, hh: (xx - 1, hh), "down" + name),
            whole(over, lambda zz, yy, xx, hh: (xx + 2, hh), "over" + name),
        ]
        return mine, *got

    one = ((n,), (n,))
    cut = n // 2
    tables = [place(one), dealt(), place(((n,), (cut, cut))), [(x % 2 == side) == (zh == y % 2)]]
    starts = [sum(len(t) for t in tables[:i]) for i in range(len(tables))]
    table = jnp.stack([jnp.asarray(v, jnp.int32) for t in tables for v in t])
    queries, table = lax.optimization_barrier((queries, table))

    own = condition(queries, left_inverse, right_inverse)
    s0 = send(own, SAME, "s0")
    q0 = send(own, OPPOSITE, "q0")
    o1 = send(own, ACROSS, "o1")
    own_sib = send(own, SIBLING, "own_sib")
    stored = after(stored_rows, own).reshape(row_count, width)
    s0, q0, o1, stored = lax.optimization_barrier((s0, q0, o1, stored))
    t0 = send(q0, SAME, "t0")
    q1 = send(o1, OPPOSITE, "q1")
    s1 = send(s0, ACROSS, "s1")
    o1_sib, q0_sib, s0_sib = send(o1, SIBLING, "o1_sib"), send(q0, SIBLING, "q0_sib"), send(s0, SIBLING, "s0_sib")
    scores_o = score_group(table, starts[0], [own, o1, own_sib, o1_sib], stored)

    t0, q1, s1, scores_o, s0_sib = lax.optimization_barrier((t0, q1, s1, scores_o, s0_sib))
    first, second = split(q1, t0, cut)
    t1a, t1b = send(first, SAME, "t1a"), send(second, ACROSS, "t1b")
    q1_sib, s1_sib, t0_sib = send(q1, SIBLING, "q1_sib"), send(s1, SIBLING, "s1_sib"), send(t0, SIBLING, "t0_sib")
    dealt_1 = score_group(table, starts[0], [q0, q1, q0_sib, q1_sib], stored, scores_o, starts[1])
    *dealt_1, s1_sib, t0_sib = lax.optimization_barrier((*dealt_1, s1_sib, t0_sib))
    mine, up, down, over = reduce_batch(dealt_1, "_oq")
    scores_s = score_group(table, starts[0], [after(s0, *dealt_1), s1, s0_sib, s1_sib], stored)
    t1a, t1b, scores_s, up, down = lax.optimization_barrier((t1a, t1b, scores_s, up, down))
    t1a_sib, t1b_sib = send(t1a, SIBLING, "t1a_sib"), send(t1b, SIBLING, "t1b_sib")
    keep_1, onward_1 = sum_blocks([mine, up, down, over])
    last = [t0, t1a, t1b, t0_sib, t1a_sib, t1b_sib]
    dealt_2 = score_group(
        table, starts[2], last, stored, scores_s, starts[1], parts=2
    )
    keep_2, onward_2 = sum_blocks(reduce_batch(dealt_2[0::2], "_st"))
    keep_3, onward_3 = sum_blocks(reduce_batch(dealt_2[1::2], "_st_right"), with_norms=False)

    def final_first(yy, xx, hh):
        return (xx % 2 == yy // 2) == (hh == yy % 2)

    def other(zz, yy, xx, hh):
        return (xx, 1 - hh) if final_first(yy, xx, hh) else None

    got_1 = whole(
        onward_1, lambda zz, yy, xx, hh: None if final_first(yy, xx, hh) else (xx, 1 - hh), "oq"
    )
    got_2 = whole(onward_2, other, "st")
    got_3 = whole(onward_3, other, "st_right")
    late = [(keep_2, got_2), (keep_3, got_3)]
    return finish(table, starts[3], late, [(keep_1, got_1)], row_count)


def solution(mesh):
    in_specs = (
        P("rows", "layers", None),
        P("rows", "layers", None),
        P("layers", None, None),
        P("layers", None, None),
    )
    out_specs = P("layers", "rows")
    return jax.shard_map(
        per_device, mesh=mesh, in_specs=in_specs, out_specs=out_specs, check_vma=False
    )
```

```python
import functools

import jax
import jax.numpy as jnp
from jax import lax
from jax.experimental import pallas as pl
from jax.experimental.pallas import tpu as pltpu
from jax.sharding import PartitionSpec as P

EPS = 1e-06
BF = jnp.bfloat16
F32 = jnp.float32
PAD = 128
MIB = 1 << 20

Z, Y, C, X, ZH = 2, 4, 2, 4, 2
BOTH = ("rows", "layers")


def rows_index(z, y, c):
    return (z * Y + y % Y) * C + c


def rows_perm(move):
    pairs = []
    for z in range(Z):
        for y in range(Y):
            for c in range(C):
                pairs.append((rows_index(z, y, c), rows_index(*move(z, y, c))))
    return pairs


SAME = rows_perm(lambda z, y, c: (z, y ^ 1, c))
OPPOSITE = rows_perm(lambda z, y, c: (z, y - 1 if y % 2 == 0 else y + 1, c))
ACROSS = rows_perm(lambda z, y, c: (1 - z, y, c))
SIBLING = rows_perm(lambda z, y, c: (z, y, 1 - c))


def whole_perm(move):
    pairs = []
    for z in range(Z):
        for y in range(Y):
            for c in range(C):
                for x in range(X):
                    for zh in range(ZH):
                        to = move(z, y, x, zh)
                        if to is not None:
                            r = rows_index(z, y, c)
                            source = r * X * ZH + x * ZH + zh
                            target = r * X * ZH + (to[0] % X) * ZH + to[1]
                            pairs.append((source, target))
    return pairs


def norm_columns(norms):
    count = norms.shape[0]
    high = norms.astype(BF).astype(F32)
    low = norms - high
    lane = lax.broadcasted_iota(jnp.int32, (count, PAD), 1)
    return jnp.where(lane < PAD // 2, high, low).astype(BF)


def thirds(value):
    parts = []
    for _ in range(3):
        parts.append(value.astype(BF))
        value = value - parts[-1].astype(F32)
    return parts


def dot(a, b):
    return lax.dot_general(a, b, (((1,), (0,)), ((), ())), preferred_element_type=F32)


def condition_kernel(q, left, right, out, back, turned_left):
    count, layers = out.shape[0], q.shape[0]
    width = q.shape[1] * q.shape[2] // count
    side = right.shape[1]
    four = 4 * side
    tiles = width // 128
    row = lax.broadcasted_iota(jnp.int32, (four, four), 0)
    col = lax.broadcasted_iota(jnp.int32, (four, four), 1)
    right_mask = row // side == col // side
    left_mask = row % 128 // 32 == col % 128 // 32
    total = jnp.zeros((count, 128), F32)
    for l in range(layers):
        lanes = jnp.concatenate([right[l]] * 4, axis=1)
        wide_r = jnp.where(right_mask, jnp.concatenate([lanes] * 4, axis=0), 0.0)
        once = dot(jnp.concatenate([q[l]] * 3, axis=1), jnp.concatenate(thirds(wide_r)[::-1], axis=0))
        quarter = side // 4

        def spread(slot, order):
            return [turned_left[slot, pl.ds(i, quarter, stride=4), :] for i in order]

        turned_left[0] = jnp.concatenate([left[l]] * 2, axis=1)
        low, high = (turned_left[0, pl.ds(i, side // 2, stride=2), :] for i in range(2))
        turn = jnp.concatenate([low] * 4 + [high] * 4, axis=0).T[:side]
        turned_left[1] = turn[:, :128]
        turned_left[2] = turn[:, 128:]
        rows = [jnp.concatenate(p, axis=1) for p in zip(spread(1, (0, 2, 1, 3)), spread(2, (0, 2, 1, 3)))]
        low, high = jnp.concatenate(rows[:2], axis=0), jnp.concatenate(rows[2:], axis=0)
        wide_l = jnp.where(left_mask, jnp.concatenate([low] * 4 + [high] * 4, axis=0), 0.0)
        stack = []
        groups = width // four
        for j in range(count // 4):
            pieces = []
            for i in range(4):
                mine = once[groups * (4 * j + i) : groups * (4 * j + i + 1)]
                pieces += [mine[:, :128], mine[:, 128:]]
            block = jnp.concatenate(pieces, axis=0).T
            stack.append(jnp.concatenate([block[:side], block[side:]], axis=1))
        turned = thirds(jnp.concatenate(stack, axis=0))
        factor = thirds(wide_l)
        terms = ((1, 1), (0, 2), (2, 0), (0, 1), (1, 0), (0, 0))
        second = dot(
            jnp.concatenate([turned[i] for i, _ in terms], axis=1),
            jnp.concatenate([factor[k] for _, k in terms], axis=0),
        )
        for j in range(count // 4):
            piece = second[side * j : side * (j + 1)]
            block = jnp.concatenate([piece[:, :128], piece[:, 128:]], axis=0).T
            for i in range(4):
                back[4 * j + i] = block[32 * i : 32 * (i + 1)]
        for t in range(tiles):
            done = back[:, t, :].astype(BF)
            out[:, l * width + 128 * t : l * width + 128 * (t + 1)] = done
            wide = done.astype(F32)
            total = total + wide * wide
    out[:, layers * width :] = norm_columns(jnp.sum(total, axis=1, keepdims=True))


def condition(queries, left, right):
    count, layers, width = queries.shape
    side = left.shape[1]
    four = 4 * side
    q = jnp.transpose(queries.reshape(count, layers, width // four, four), (1, 0, 2, 3))
    vmem = pl.BlockSpec(memory_space=pltpu.VMEM)
    return pl.pallas_call(
        condition_kernel,
        out_shape=jax.ShapeDtypeStruct((count, layers * width + PAD), BF),
        in_specs=[vmem] * 3,
        out_specs=vmem,
        scratch_shapes=[
            pltpu.VMEM((count, width // 128, 128), F32),
            pltpu.VMEM((3, side, 128), F32),
        ],
        compiler_params=pltpu.CompilerParams(vmem_limit_bytes=24 * MIB),
        name="condition",
    )(q.reshape(layers, count * width // four, four), left, right)


def fill(at, place, pieces, group):
    for i, piece in enumerate(pieces):
        rows = piece.shape[0]
        group[pl.ds(pl.multiple_of(place[at + i], 16), rows), :] = piece[...]


def products(group, stored):
    width = stored.shape[1]
    return lax.dot_general(
        group[:, :width], stored[...], (((1,), (1,)), ((), ())), preferred_element_type=F32
    )


def score_kernel(at, place, *refs):
    *pieces, stored, scores, group = refs
    edge = scores.shape[1] - PAD
    fill(at, place, pieces, group)
    scores[:, :edge] = products(group, stored).astype(BF)
    scores[:, edge:] = group[:, stored.shape[1] :]


def deal_kernel(at, deal, parts, count, place, *refs):
    pieces, stored, before = refs[:count], refs[count], refs[count + 1]
    outs, (group, blocks) = refs[count + 2 : -2], refs[-2:]
    edge = before.shape[1] - PAD
    rows = before.shape[0]
    fill(at, place, pieces, group)
    blocks[:rows] = before[...]
    blocks[rows:, :edge] = products(group, stored).astype(BF)
    blocks[rows:, edge:] = group[:, stored.shape[1] :]
    size = rows // 2
    for j in range(4):
        take = pl.ds(pl.multiple_of(place[deal + j] * size, 128), size)
        if parts == 1:
            outs[j][...] = blocks[take, :]
        else:
            first, second = outs[2 * j], outs[2 * j + 1]
            cut = second.shape[1]
            first[:, :cut] = blocks[take, :cut]
            first[:, cut:] = blocks[take, edge:]
            second[...] = blocks[take, cut:edge]


def score_group(place, at, pieces, stored, before=None, deal=None, parts=1):
    count, width = stored.shape
    rows = sum(p.shape[0] for p in pieces)
    vmem = pl.BlockSpec(memory_space=pltpu.VMEM)
    scratch = [pltpu.VMEM((rows, width + PAD), BF)]
    shape = jax.ShapeDtypeStruct((rows, count + PAD), BF)
    more = []
    if before is None:
        kernel, name = functools.partial(score_kernel, at), "score_group"
        out, out_specs = shape, vmem
    else:
        kernel, name = functools.partial(deal_kernel, at, deal, parts, len(pieces)), "score_and_deal"
        widths = [count + PAD] if parts == 1 else [count // 2 + PAD, count // 2]
        out = [jax.ShapeDtypeStruct((rows // 2, w), BF) for w in widths] * 4
        out_specs = [vmem] * len(out)
        scratch.append(pltpu.VMEM((2 * rows, count + PAD), BF))
        more = [before]
    return pl.pallas_call(
        kernel,
        out_shape=out,
        in_specs=[pl.BlockSpec(memory_space=pltpu.SMEM)] + [vmem] * (len(pieces) + 1 + len(more)),
        out_specs=out_specs,
        scratch_shapes=scratch,
        compiler_params=pltpu.CompilerParams(vmem_limit_bytes=12 * MIB),
        cost_estimate=pl.CostEstimate(
            flops=2 * rows * width * count, bytes_accessed=2 * count * width, transcendentals=0
        ),
        name=name,
    )(place, *pieces, stored, *more)


def sum_kernel(v, a, b, c, keep, onward):
    edge = v.shape[1] - PAD
    total = v[...].astype(F32) + a[...].astype(F32) + b[...].astype(F32) + c[...].astype(F32)
    norms = total[:, edge : edge + 1] + total[:, edge + PAD // 2 : edge + PAD // 2 + 1]
    keep[:, :edge] = total[:, :edge]
    keep[:, edge:] = jnp.broadcast_to(norms, (v.shape[0], PAD))
    onward[:, :edge] = total[:, :edge].astype(BF)
    onward[:, edge:] = norm_columns(norms)


def plain_kernel(v, a, b, c, keep, onward):
    total = v[...].astype(F32) + a[...].astype(F32) + b[...].astype(F32) + c[...].astype(F32)
    keep[...] = total
    onward[...] = total.astype(BF)


def sum_blocks(blocks, with_norms=True):
    shape = blocks[0].shape
    vmem = pl.BlockSpec(memory_space=pltpu.VMEM)
    return pl.pallas_call(
        sum_kernel if with_norms else plain_kernel,
        out_shape=(jax.ShapeDtypeStruct(shape, F32), jax.ShapeDtypeStruct(shape, BF)),
        in_specs=[vmem] * 4,
        out_specs=(vmem, vmem),
        compiler_params=pltpu.CompilerParams(vmem_limit_bytes=6 * MIB),
        name="sum_blocks",
    )(*blocks)


def finish_kernel(at, which, *refs):
    *parts, out = refs

    def scale(keep, got):
        edge = keep.shape[1] - PAD
        more = got[:, edge:].astype(F32)
        norms = keep[:, edge : edge + 1] + (more[:, :1] + more[:, PAD // 2 : PAD // 2 + 1])
        return lax.rsqrt(norms + EPS)

    def write(pairs):
        by = scale(*pairs[0])
        start = 0
        for i, (keep, got) in enumerate(pairs):
            stop = start + keep.shape[1] - (PAD if i == 0 else 0)
            out[:, start:stop] = (keep[:, : stop - start] + got[:, : stop - start].astype(F32)) * by
            start = stop

    pl.when(which[at] == 0)(lambda: write([parts[0:2], parts[2:4]]))
    pl.when(which[at] != 0)(lambda: write([parts[4:6]]))


def finish(which, at, late, early, columns):
    vmem = pl.BlockSpec(memory_space=pltpu.VMEM)
    arrays = [array for pair in (*late, *early) for array in pair]
    return pl.pallas_call(
        functools.partial(finish_kernel, at),
        out_shape=jax.ShapeDtypeStruct((arrays[0].shape[0], columns), F32),
        in_specs=[pl.BlockSpec(memory_space=pltpu.SMEM)] + [vmem] * len(arrays),
        out_specs=vmem,
        compiler_params=pltpu.CompilerParams(vmem_limit_bytes=4 * MIB),
        name="finish",
    )(which, *arrays)


def split_kernel(a, b, first, second):
    count = first.shape[0]
    first[...] = a[:count]
    second[...] = b[count:]


def split(a, b, count):
    vmem = pl.BlockSpec(memory_space=pltpu.VMEM)
    return pl.pallas_call(
        split_kernel,
        out_shape=[jax.ShapeDtypeStruct((size, a.shape[1]), a.dtype) for size in (count, b.shape[0] - count)],
        in_specs=[vmem] * 2,
        out_specs=[vmem] * 2,
        compiler_params=pltpu.CompilerParams(vmem_limit_bytes=4 * MIB),
        name="split",
    )(a, b)


def after(value, *others):
    return lax.optimization_barrier((value, *others))[0]


def per_device(queries, stored_rows, left_inverse, right_inverse):
    row_count = stored_rows.shape[0]
    width = stored_rows.shape[1] * stored_rows.shape[2]
    n = queries.shape[0]
    rows_at = lax.axis_index("rows")
    layers_at = lax.axis_index("layers")
    z, y, core = rows_at // (Y * C), (rows_at // C) % Y, rows_at % C
    x, zh = layers_at // ZH, layers_at % ZH
    side = y // 2

    def send(value, pairs, name):
        with jax.named_scope(name):
            return lax.ppermute(value, "rows", pairs)

    def whole(value, move, name):
        with jax.named_scope(name):
            return lax.ppermute(value, BOTH, whole_perm(move))

    def place(rows_of):
        offsets = []
        for at in (core, 1 - core):
            for block, rows in enumerate(rows_of):
                start = 2 * n * block + n * at
                for count in rows:
                    offsets.append(start)
                    start = start + count
        return offsets

    def dealt():
        to = [(x + step) % X for step in (0, 1, 2, 3)]
        return [2 * (t % 2 != side) + (t // 2 != z) for t in to]

    def reduce_batch(blocks, name):
        mine, up, over, down = blocks
        got = [
            whole(up, lambda zz, yy, xx, hh: (xx + 1, hh), "up" + name),
            whole(down, lambda zz, yy, xx, hh: (xx - 1, hh), "down" + name),
            whole(over, lambda zz, yy, xx, hh: (xx + 2, hh), "over" + name),
        ]
        return mine, *got

    one = ((n,), (n,))
    cut = n // 2
    tables = [place(one), dealt(), place(((n,), (cut, cut))), [(x % 2 == side) == (zh == y % 2)]]
    starts = [sum(len(t) for t in tables[:i]) for i in range(len(tables))]
    table = jnp.stack([jnp.asarray(v, jnp.int32) for t in tables for v in t])
    queries, table = lax.optimization_barrier((queries, table))

    own = condition(queries, left_inverse, right_inverse)
    s0 = send(own, SAME, "s0")
    q0 = send(own, OPPOSITE, "q0")
    o1 = send(own, ACROSS, "o1")
    own_sib = send(own, SIBLING, "own_sib")
    stored = after(stored_rows, own).reshape(row_count, width)
    s0, q0, o1, stored = lax.optimization_barrier((s0, q0, o1, stored))
    t0 = send(q0, SAME, "t0")
    q1 = send(o1, OPPOSITE, "q1")
    s1 = send(s0, ACROSS, "s1")
    o1_sib, q0_sib, s0_sib = send(o1, SIBLING, "o1_sib"), send(q0, SIBLING, "q0_sib"), send(s0, SIBLING, "s0_sib")
    scores_o = score_group(table, starts[0], [own, o1, own_sib, o1_sib], stored)

    t0, q1, s1, scores_o, s0_sib = lax.optimization_barrier((t0, q1, s1, scores_o, s0_sib))
    first, second = split(q1, t0, cut)
    t1a, t1b = send(first, SAME, "t1a"), send(second, ACROSS, "t1b")
    q1_sib, s1_sib, t0_sib = send(q1, SIBLING, "q1_sib"), send(s1, SIBLING, "s1_sib"), send(t0, SIBLING, "t0_sib")
    dealt_1 = score_group(table, starts[0], [q0, q1, q0_sib, q1_sib], stored, scores_o, starts[1])
    *dealt_1, s1_sib, t0_sib = lax.optimization_barrier((*dealt_1, s1_sib, t0_sib))
    mine, up, down, over = reduce_batch(dealt_1, "_oq")
    scores_s = score_group(table, starts[0], [after(s0, *dealt_1), s1, s0_sib, s1_sib], stored)
    t1a, t1b, scores_s, up, down = lax.optimization_barrier((t1a, t1b, scores_s, up, down))
    t1a_sib, t1b_sib = send(t1a, SIBLING, "t1a_sib"), send(t1b, SIBLING, "t1b_sib")
    keep_1, onward_1 = sum_blocks([mine, up, down, over])
    last = [t0, t1a, t1b, t0_sib, t1a_sib, t1b_sib]
    dealt_2 = score_group(
        table, starts[2], last, stored, scores_s, starts[1], parts=2
    )
    keep_2, onward_2 = sum_blocks(reduce_batch(dealt_2[0::2], "_st"))
    keep_3, onward_3 = sum_blocks(reduce_batch(dealt_2[1::2], "_st_right"), with_norms=False)

    def final_first(yy, xx, hh):
        return (xx % 2 == yy // 2) == (hh == yy % 2)

    def other(zz, yy, xx, hh):
        return (xx, 1 - hh) if final_first(yy, xx, hh) else None

    got_1 = whole(
        onward_1, lambda zz, yy, xx, hh: None if final_first(yy, xx, hh) else (xx, 1 - hh), "oq"
    )
    got_2 = whole(onward_2, other, "st")
    got_3 = whole(onward_3, other, "st_right")
    late = [(keep_2, got_2), (keep_3, got_3)]
    return finish(table, starts[3], late, [(keep_1, got_1)], row_count)


def solution(mesh):
    in_specs = (
        P("rows", "layers", None),
        P("rows", "layers", None),
        P("layers", None, None),
        P("layers", None, None),
    )
    out_specs = P("layers", "rows")
    return jax.shard_map(
        per_device, mesh=mesh, in_specs=in_specs, out_specs=out_specs, check_vma=False
    )
```
